128 devices in a mesh: row: 16 (over z_hi, x, core), col: 8 (over z_lo, y).
Axes of the slice: x: 4, y: 4, z: 4 (z_hi: 2, z_lo: 2; z = z_hi * 2 + z_lo), core: 2. Of those that a mesh axis runs over, the one named last changes fastest.
Arguments:
- pair: bfloat16 [512, 512, 128], P('row', 'col'), may hold values from -6 to 6
- in_gain: float32 [128], replicated, may hold values from 0.1 to 1.9
- in_bias: float32 [128], replicated, may hold values from -3 to 3
- a_gate: bfloat16 [128, 128], replicated, may hold values from -0.5 to 0.5
- a_proj: bfloat16 [128, 128], replicated, may hold values from -0.5 to 0.5
- b_gate: bfloat16 [128, 128], replicated, may hold values from -0.5 to 0.5
- b_proj: bfloat16 [128, 128], replicated, may hold values from -0.5 to 0.5
- out_gate: bfloat16 [128, 128], replicated, may hold values from -0.5 to 0.5
- mid_gain: float32 [128], replicated, may hold values from 0.1 to 1.9
- mid_bias: float32 [128], replicated, may hold values from -3 to 3
- out_proj: bfloat16 [128, 128], replicated, may hold values from -0.5 to 0.5
Outputs:
- update: bfloat16 [512, 512, 128], P('row', 'col')
The draws below stay inside these ranges and needn't reach their ends.
All inputs are finite; a program needn't handle non-finite values.
Results may differ from the reference program's by a relative error of at most 0.0054.
Values may be sent and summed in bfloat16 or wider, within the bound.
No kernel may reach another device: no remote copies, remote signals or barrier semaphores. Data moves between devices by JAX's collectives and lax.ppermute only.
A program may use at most 128 MiB of HBM per device.

```python
import jax
import jax.numpy as jnp
from jax import lax

C = 128
HID = 128
ROW_DEV = 32
N = 512


def levels(stream_key, shape, split, smallest, top_value):
    loudness, own = 1.0, jax.random.fold_in(stream_key, 6)
    for axis_at, shards_of in split:
        heights = jnp.exp(jax.random.uniform(jax.random.fold_in(own, axis_at), (shards_of,), jnp.float32, smallest / len(split), top_value / len(split)))
        loudness = loudness * jnp.repeat(heights, shape[axis_at] // shards_of).reshape([-1 if axis == axis_at else 1 for axis in range(len(shape))])
    return loudness


def gaussian(key, shape, scale, reach, cuts=(), dtype=jnp.bfloat16):
    drawn = jax.random.normal(key, shape, jnp.float32) * scale
    if len(cuts) > 0:
        drawn = levels(key, shape, cuts, -0.22, 0.18) * drawn
    return jnp.clip(drawn, min=-reach, max=reach).astype(dtype)


def setup_inputs(seed: int = 0) -> dict:
    streams_of = jax.random.split(jax.random.key(seed), 12)
    return {
        "pair": gaussian(streams_of[0], (N, N, C), 1.0, 6.0, ((0, 16), (1, 8))),
        "in_gain": jnp.clip(1.0 + 0.18 * jax.random.normal(streams_of[1], (C,), jnp.float32), 0.1, 1.9),
        "in_bias": gaussian(streams_of[2], (C,), 0.5, 3.0, (), jnp.float32),
        "a_gate": gaussian(streams_of[3], (C, HID), C ** -0.5, 0.5),
        "a_proj": gaussian(streams_of[4], (C, HID), C ** -0.5, 0.5),
        "b_gate": gaussian(streams_of[5], (C, HID), C ** -0.5, 0.5),
        "b_proj": gaussian(streams_of[6], (C, HID), C ** -0.5, 0.5),
        "out_gate": gaussian(streams_of[7], (C, C), C ** -0.5, 0.5),
        "mid_gain": jnp.clip(1.0 + 0.18 * jax.random.normal(streams_of[8], (HID,), jnp.float32), 0.1, 1.9),
        "mid_bias": gaussian(streams_of[9], (HID,), 0.5, 3.0, (), jnp.float32),
        "out_proj": gaussian(streams_of[10], (HID, C), HID ** -0.5, 0.5),
    }


def layer_norm(values, gain, bias):
    mean = lax.optimization_barrier(jnp.mean(values, axis=-1, keepdims=True))
    centered = values - mean
    variance = lax.optimization_barrier(jnp.mean(centered * centered, axis=-1, keepdims=True))
    return centered * lax.rsqrt(variance + 1e-05) * gain + bias

def reference(pair, in_gain, in_bias, a_gate, a_proj, b_gate, b_proj, out_gate, mid_gain, mid_bias, out_proj):
    normed = layer_norm(pair.astype(jnp.float32), in_gain, in_bias).astype(jnp.bfloat16)
    flat = normed.reshape(N * N, C)

    def project(weight):
        return jnp.dot(flat, weight, preferred_element_type=jnp.float32).reshape(N, N, weight.shape[1])
    left = (jax.nn.sigmoid(project(a_gate)) * project(a_proj)).astype(jnp.bfloat16)
    right = (jax.nn.sigmoid(project(b_gate)) * project(b_proj)).astype(jnp.bfloat16)
    gate = jax.nn.sigmoid(project(out_gate))
    left_wide = left.astype(jnp.float32)
    right_wide = right.astype(jnp.float32)

    def block_rows(rows):
        return jnp.einsum('ikc,jkc->ijc', rows, right_wide)
    triangle = lax.map(block_rows, left_wide.reshape(N // ROW_DEV, ROW_DEV, N, HID)).reshape(N, N, HID)
    mixed = layer_norm(triangle, mid_gain, mid_bias).astype(jnp.bfloat16)
    output = jnp.dot(mixed.reshape(N * N, HID), out_proj, preferred_element_type=jnp.float32).reshape(N, N, C)
    return (gate * output).astype(jnp.bfloat16)
```

```python
import jax
import jax.numpy as jnp
from jax import lax
from jax.experimental import pallas as pl
from jax.experimental.pallas import tpu as pltpu
from jax.sharding import PartitionSpec as P

BF16, F32 = jnp.bfloat16, jnp.float32
EPS = 1e-05
BOTH = ("row", "col")


def sigmoid(x):
    return 0.5 + 0.5 * jnp.tanh(0.5 * x)


def identity(size):
    return (
        lax.broadcasted_iota(jnp.int32, (size, size), 0)
        == lax.broadcasted_iota(jnp.int32, (size, size), 1)
    ).astype(BF16)


def dot(a, b, contract):
    return lax.dot_general(a, b, ((contract[:1], contract[1:]), ((), ())), preferred_element_type=F32)


def column(vector, width):
    return jnp.broadcast_to(vector, (width, vector.shape[1])).T


def norm(values, axis):
    mean = jnp.mean(values, axis=axis, keepdims=True)
    centered = values - mean
    variance = jnp.mean(centered * centered, axis=axis, keepdims=True)
    return centered * lax.rsqrt(variance + EPS)


def operands_kernel(pair_ref, gain_ref, bias_ref, ag_ref, ap_ref, bg_ref, bp_ref, out_ref, wide_ref):
    rows, cols, chans = pair_ref.shape
    half = rows // 2
    tiles = 2 * half
    eye = identity(chans)
    gain, bias = column(gain_ref[...], 2 * cols), column(bias_ref[...], 2 * cols)
    weights = [ref[...].T for ref in (ag_ref, ap_ref, bg_ref, bp_ref)]
    for s in range(half):
        block = jnp.concatenate([pair_ref[s], pair_ref[half + s]], axis=0)
        turned = dot(eye, block, (1, 1))
        normed = (norm(turned, 0) * gain + bias).astype(BF16)
        a_gate, a_proj, b_gate, b_proj = (dot(w, normed, (1, 0)) for w in weights)
        wide_ref[pl.ds(s, chans, stride=tiles), :] = sigmoid(a_gate) * a_proj
        wide_ref[pl.ds(half + s, chans, stride=tiles), :] = sigmoid(b_gate) * b_proj
    out_ref[...] = wide_ref[...].astype(BF16).reshape(out_ref.shape)


def gate_kernel(pair_ref, gain_ref, bias_ref, weight_ref, out_ref):
    rows, cols, chans = pair_ref.shape
    values = pair_ref[...].reshape(rows * cols, chans).astype(F32)
    normed = (norm(values, 1) * gain_ref[...] + bias_ref[...]).astype(BF16)
    out_ref[...] = sigmoid(dot(normed, weight_ref[...], (1, 0))).reshape(out_ref.shape)


def product_kernel(in_ref, out_ref, left_ref, right_ref):
    row_count, col_count, lanes = in_ref.shape[0], in_ref.shape[1], in_ref.shape[3]
    tile = in_ref.shape[2] // 2
    cols = lanes // 2
    groups = row_count * tile
    for m in range(col_count // 2):
        for which, ref in ((0, left_ref), (1, right_ref)):
            part = pl.ds(which * tile, tile)
            even = in_ref[:, 2 * m, part, :]
            odd = in_ref[:, 2 * m + 1, part, :]
            for h in range(2):
                ref[:, h, :, m * lanes : (m + 1) * lanes] = jnp.concatenate(
                    [even[:, :, h * cols : (h + 1) * cols], odd[:, :, h * cols : (h + 1) * cols]], axis=2
                )
    depth = right_ref.shape[3]
    right = right_ref[...].reshape(2 * groups, depth)
    products = [
        dot(left_ref[:, h].reshape(groups, depth), right, (1, 1)).astype(BF16).reshape(row_count, tile, 2 * groups)
        for h in range(2)
    ]
    for m in range(col_count // 2):
        first, second = (p[:, :, m * lanes : (m + 1) * lanes] for p in products)
        for odd in range(2):
            cut = slice(odd * cols, (odd + 1) * cols)
            out_ref[:, 2 * m + odd] = jnp.concatenate(
                [first[:, :, cut], second[:, :, cut]], axis=2
            )


def update_kernel(in_ref, gate_ref, gain_ref, bias_ref, weight_ref, out_ref, wide_ref):
    chans, half, lanes = in_ref.shape
    cols = lanes // 2
    gain, bias = column(gain_ref[...], lanes), column(bias_ref[...], lanes)
    wide_ref[...] = norm(in_ref[...].astype(F32), 0).reshape(wide_ref.shape)
    for s in range(half):
        mixed = (wide_ref[pl.ds(s, chans, stride=half), :] * gain + bias).astype(BF16)
        output = dot(mixed, weight_ref[...], (0, 0))
        out_ref[s] = (gate_ref[s] * output[:cols]).astype(BF16)
        out_ref[half + s] = (gate_ref[half + s] * output[cols:]).astype(BF16)


VMEM_LIMIT = 48 * 2**20


def call(kernel, out, scratch=(), flops=0):
    return pl.pallas_call(
        kernel,
        out_shape=out,
        scratch_shapes=list(scratch),
        compiler_params=pltpu.CompilerParams(vmem_limit_bytes=VMEM_LIMIT),
        cost_estimate=pl.CostEstimate(flops=flops, bytes_accessed=2**20, transcendentals=2**18),
    )


def per_device(
    pair, in_gain, in_bias, a_gate, a_proj, b_gate, b_proj, out_gate, mid_gain, mid_bias, out_proj
):
    rows, cols, chans = pair.shape
    hidden = a_gate.shape[1]
    row_count, col_count = lax.axis_size("row"), lax.axis_size("col")
    half, lanes = rows // 2, 2 * cols
    gain, bias = in_gain[None, :], in_bias[None, :]
    operands = call(
        operands_kernel,
        jax.ShapeDtypeStruct((hidden, 2 * half, lanes), BF16),
        [pltpu.VMEM((hidden * 2 * half, lanes), F32)],
        2 * rows * cols * chans * 4 * hidden,
    )(pair, gain, bias, a_gate, a_proj, b_gate, b_proj)
    channel = lax.all_to_all(operands, BOTH, 0, 0, tiled=True)
    gate = call(gate_kernel, jax.ShapeDtypeStruct(pair.shape, F32), (), 2 * rows * cols * chans * chans)(
        pair, gain, bias, out_gate
    )
    count, depth = row_count * half, col_count * cols
    triangle = call(
        product_kernel,
        jax.ShapeDtypeStruct((row_count, col_count, half, lanes), BF16),
        [pltpu.VMEM((row_count, 2, half, depth), BF16), pltpu.VMEM((row_count, 2, half, depth), BF16)],
        8 * count * count * depth,
    )(channel.reshape(row_count, col_count, 2 * half, lanes))
    triangle = lax.all_to_all(triangle.reshape(operands.shape[0], half, lanes), BOTH, 0, 0, tiled=True)
    return call(
        update_kernel,
        jax.ShapeDtypeStruct(pair.shape, BF16),
        [pltpu.VMEM((hidden * half, lanes), F32)],
        2 * rows * cols * hidden * chans,
    )(triangle, gate, mid_gain[None, :], mid_bias[None, :], out_proj)


def solution(mesh):
    in_specs = (P("row", "col", None), P(), P(), P(), P(), P(), P(), P(), P(), P(), P())
    return jax.shard_map(
        per_device, mesh=mesh, in_specs=in_specs, out_specs=P("row", "col", None), check_vma=False
    )
```

```python
import jax
import jax.numpy as jnp
from jax import lax
from jax.experimental import pallas as pl
from jax.experimental.pallas import tpu as pltpu
from jax.sharding import PartitionSpec as P

BF16, F32 = jnp.bfloat16, jnp.float32
EPS = 1e-05
BOTH = ("row", "col")


def sigmoid(x):
    return 0.5 + 0.5 * jnp.tanh(0.5 * x)


def identity(size):
    return (
        lax.broadcasted_iota(jnp.int32, (size, size), 0)
        == lax.broadcasted_iota(jnp.int32, (size, size), 1)
    ).astype(BF16)


def dot(a, b, contract):
    return lax.dot_general(a, b, ((contract[:1], contract[1:]), ((), ())), preferred_element_type=F32)


def column(vector, width):
    return jnp.broadcast_to(vector, (width, vector.shape[1])).T


def norm(values, axis):
    mean = jnp.mean(values, axis=axis, keepdims=True)
    centered = values - mean
    variance = jnp.mean(centered * centered, axis=axis, keepdims=True)
    return centered * lax.rsqrt(variance + EPS)


def start(copies):
    for copy in copies:
        copy.start()
    return copies


def wait(copies):
    for copy in copies:
        copy.wait()


def operands_kernel(
    pair_hbm, gain_hbm, bias_hbm, ag_hbm, ap_hbm, bg_hbm, bp_hbm, out_ref, pair_ref, vector_ref, weight_ref, wide_ref, sem
):
    rows, _, chans = pair_hbm.shape
    half = rows // 2
    small = [pltpu.make_async_copy(ref, weight_ref.at[n], sem.at[n]) for n, ref in enumerate((ag_hbm, ap_hbm, bg_hbm, bp_hbm))]
    small += [pltpu.make_async_copy(ref, vector_ref.at[pl.ds(n, 1)], sem.at[4 + n]) for n, ref in enumerate((gain_hbm, bias_hbm))]
    start(small)
    step = half // PARTS
    parts = []
    for n in range(PARTS):
        spans = [pl.ds(h * half + n * step, step) for h in range(2)]
        parts.append(
            start([pltpu.make_async_copy(pair_hbm.at[at], pair_ref.at[at], sem.at[6 + 2 * n + h]) for h, at in enumerate(spans)])
        )
    eye = identity(chans)
    wait(small)
    weights = jnp.concatenate([weight_ref[n].T for n in range(4)], axis=0)
    gain, bias = (jnp.concatenate([column(vector_ref[n : n + 1], LANES)] * 2, axis=1) for n in range(2))
    pitch = 2 * half + 1
    for s in range(0, half, 2):
        if s % step == 0:
            wait(parts[s // step])
        block = jnp.concatenate([pair_ref[row] for row in (s, half + s, s + 1, half + s + 1)], axis=0)
        normed = (norm(dot(eye, block, (1, 1)), 0) * gain + bias).astype(BF16)
        projected = dot(weights, normed, (1, 0))
        a_gate, a_proj, b_gate, b_proj = (projected[n * chans : (n + 1) * chans] for n in range(4))
        left, right = sigmoid(a_gate) * a_proj, sigmoid(b_gate) * b_proj
        for n in range(2):
            cut = slice(n * LANES, (n + 1) * LANES)
            wide_ref[pl.ds(s + n, chans, stride=pitch), :] = left[:, cut]
            wide_ref[pl.ds(half + s + n, chans, stride=pitch), :] = right[:, cut]
    for c in range(chans):
        out_ref[c] = wide_ref[pl.ds(c * pitch, 2 * half), :].astype(BF16)


def gate_kernel(
    pair_hbm, gain_hbm, bias_hbm, weight_hbm, mid_gain_hbm, mid_bias_hbm, out_proj_hbm,
    out_ref, mid_gain_ref, mid_bias_ref, out_proj_ref, pair_ref, vector_ref, weight_ref, sem,
):
    rows, cols, chans = pair_hbm.shape
    copies = [
        pltpu.make_async_copy(pair_hbm, pair_ref, sem.at[0]),
        pltpu.make_async_copy(weight_hbm, weight_ref, sem.at[1]),
        pltpu.make_async_copy(out_proj_hbm, out_proj_ref, sem.at[2]),
    ]
    vectors = (gain_hbm, bias_hbm, mid_gain_hbm, mid_bias_hbm)
    copies += [pltpu.make_async_copy(ref, vector_ref.at[pl.ds(n, 1)], sem.at[3 + n]) for n, ref in enumerate(vectors)]
    wait(start(copies))
    mid_gain_ref[...] = column(vector_ref[2:3], LANES)
    mid_bias_ref[...] = column(vector_ref[3:4], LANES)
    values = pair_ref[...].reshape(rows * cols, chans).astype(F32)
    normed = (norm(values, 1) * vector_ref[0:1] + vector_ref[1:2]).astype(BF16)
    out_ref[...] = sigmoid(dot(normed, weight_ref[...], (1, 0))).reshape(out_ref.shape)


def product_kernel(in_ref, out_ref, left_ref, right_ref):
    row_count, col_count, lanes = in_ref.shape[0], in_ref.shape[1], in_ref.shape[3]
    tile = in_ref.shape[2] // 2
    cols = lanes // 2
    groups = row_count * tile
    for m in range(col_count // 2):
        for which, ref in ((0, left_ref), (1, right_ref)):
            part = pl.ds(which * tile, tile)
            even = in_ref[:, 2 * m, part, :]
            odd = in_ref[:, 2 * m + 1, part, :]
            for h in range(2):
                ref[:, h, :, m * lanes : (m + 1) * lanes] = jnp.concatenate(
                    [even[:, :, h * cols : (h + 1) * cols], odd[:, :, h * cols : (h + 1) * cols]], axis=2
                )
    depth = right_ref.shape[3]
    right = right_ref[...].reshape(2 * groups, depth)
    products = [
        dot(left_ref[:, h].reshape(groups, depth), right, (1, 1)).astype(BF16).reshape(row_count, tile, 2 * groups)
        for h in range(2)
    ]
    for m in range(col_count // 2):
        first, second = (p[:, :, m * lanes : (m + 1) * lanes] for p in products)
        for odd in range(2):
            cut = slice(odd * cols, (odd + 1) * cols)
            out_ref[:, 2 * m + odd] = jnp.concatenate(
                [first[:, :, cut], second[:, :, cut]], axis=2
            )


def update_kernel(in_ref, gate_ref, gain_ref, bias_ref, weight_ref, out_hbm, wide_ref, out_ref, sem):
    chans, half, lanes = in_ref.shape
    cols = lanes // 2
    pitch = half + 1
    normed = norm(in_ref[...].astype(F32), 0)
    for c in range(chans):
        wide_ref[pl.ds(c * pitch, half), :] = normed[c]
    step = half // PARTS
    copies = []
    for s in range(half):
        mixed = (wide_ref[pl.ds(s, chans, stride=pitch), :] * gain_ref[...] + bias_ref[...]).astype(BF16)
        output = dot(mixed, weight_ref[...], (0, 0))
        out_ref[s] = (gate_ref[s] * output[:cols]).astype(BF16)
        out_ref[half + s] = (gate_ref[half + s] * output[cols:]).astype(BF16)
        if s % step == step - 1:
            for h in range(2):
                at = pl.ds(h * half + s - step + 1, step)
                copies += start([pltpu.make_async_copy(out_ref.at[at], out_hbm.at[at], sem.at[len(copies)])])
    wait(copies)


LANES = 128
PARTS = 4
VMEM_LIMIT = 48 * 2**20


def in_hbm(*arrays):
    return [pltpu.with_memory_space_constraint(array, pltpu.HBM) for array in arrays]


def call(kernel, out, scratch=(), flops=0, **specs):
    return pl.pallas_call(
        kernel,
        out_shape=out,
        scratch_shapes=list(scratch),
        compiler_params=pltpu.CompilerParams(vmem_limit_bytes=VMEM_LIMIT),
        cost_estimate=pl.CostEstimate(flops=flops, bytes_accessed=2**20, transcendentals=2**18),
        **specs,
    )


def per_device(
    pair, in_gain, in_bias, a_gate, a_proj, b_gate, b_proj, out_gate, mid_gain, mid_bias, out_proj
):
    rows, cols, chans = pair.shape
    hidden = a_gate.shape[1]
    row_count, col_count = lax.axis_size("row"), lax.axis_size("col")
    half, lanes = rows // 2, 2 * cols
    hbm = pl.BlockSpec(memory_space=pltpu.HBM)
    gain, bias = in_gain[None, :], in_bias[None, :]
    operands = call(
        operands_kernel,
        jax.ShapeDtypeStruct((hidden, 2 * half, lanes), BF16),
        [
            pltpu.VMEM(pair.shape, BF16),
            pltpu.VMEM((8, chans), F32),
            pltpu.VMEM((4, chans, hidden), BF16),
            pltpu.VMEM(((hidden + 8) * (2 * half + 1), lanes), F32),
            pltpu.SemaphoreType.DMA((6 + 2 * PARTS,)),
        ],
        2 * rows * cols * chans * 4 * hidden,
        in_specs=[hbm] * 7,
    )(*in_hbm(pair, gain, bias, a_gate, a_proj, b_gate, b_proj))
    channel = lax.all_to_all(operands, BOTH, 0, 0, tiled=True)
    gate, mid_gain, mid_bias, out_proj = call(
        gate_kernel,
        (
            jax.ShapeDtypeStruct(pair.shape, F32),
            jax.ShapeDtypeStruct((hidden, lanes), F32),
            jax.ShapeDtypeStruct((hidden, lanes), F32),
            jax.ShapeDtypeStruct(out_proj.shape, BF16),
        ),
        [
            pltpu.VMEM(pair.shape, BF16),
            pltpu.VMEM((8, chans), F32),
            pltpu.VMEM(out_gate.shape, BF16),
            pltpu.SemaphoreType.DMA((7,)),
        ],
        2 * rows * cols * chans * chans,
        in_specs=[hbm] * 7,
    )(*in_hbm(pair, gain, bias, out_gate, mid_gain[None, :], mid_bias[None, :], out_proj))
    count, depth = row_count * half, col_count * cols
    triangle = call(
        product_kernel,
        jax.ShapeDtypeStruct((row_count, col_count, half, lanes), BF16),
        [pltpu.VMEM((row_count, 2, half, depth), BF16), pltpu.VMEM((row_count, 2, half, depth), BF16)],
        8 * count * count * depth,
    )(channel.reshape(row_count, col_count, 2 * half, lanes))
    triangle = lax.all_to_all(triangle.reshape(hidden, half, lanes), BOTH, 0, 0, tiled=True)
    return call(
        update_kernel,
        jax.ShapeDtypeStruct(pair.shape, BF16),
        [
            pltpu.VMEM(((hidden + 8) * (half + 1), lanes), F32),
            pltpu.VMEM(pair.shape, BF16),
            pltpu.SemaphoreType.DMA((2 * PARTS,)),
        ],
        2 * rows * cols * hidden * chans,
        out_specs=hbm,
    )(triangle, gate, mid_gain, mid_bias, out_proj)


def solution(mesh):
    in_specs = (P("row", "col", None), P(), P(), P(), P(), P(), P(), P(), P(), P(), P())
    return jax.shard_map(
        per_device, mesh=mesh, in_specs=in_specs, out_specs=P("row", "col", None), check_vma=False
    )
```

```python
import jax
import jax.numpy as jnp
from jax import lax
from jax.experimental import pallas as pl
from jax.experimental.pallas import tpu as pltpu
from jax.sharding import PartitionSpec as P

BF16, F32 = jnp.bfloat16, jnp.float32
EPS = 1e-05
BOTH = ("row", "col")


def sigmoid(x):
    return 0.5 + 0.5 * jnp.tanh(0.5 * x)


def centring(size):
    same = lax.broadcasted_iota(jnp.int32, (size, size), 0) == lax.broadcasted_iota(jnp.int32, (size, size), 1)
    return jnp.where(same, 1 - 1 / size, -1 / size).astype(BF16)


def dot(a, b, contract):
    return lax.dot_general(a, b, ((contract[:1], contract[1:]), ((), ())), preferred_element_type=F32)


def column(vector, width):
    return jnp.broadcast_to(vector, (width, vector.shape[1])).T


def norm(values, axis):
    mean = jnp.mean(values, axis=axis, keepdims=True)
    centered = values - mean
    variance = jnp.mean(centered * centered, axis=axis, keepdims=True)
    return centered * lax.rsqrt(variance + EPS)


def start(copies):
    for copy in copies:
        copy.start()
    return copies


def wait(copies):
    for copy in copies:
        copy.wait()


def operands_kernel(
    pair_hbm, gain_hbm, bias_hbm, ag_hbm, ap_hbm, bg_hbm, bp_hbm, out_ref, pair_ref, vector_ref, weight_ref, wide_ref, sem
):
    rows, _, chans = pair_hbm.shape
    half = rows // 2
    small = [pltpu.make_async_copy(ref, weight_ref.at[n], sem.at[n]) for n, ref in enumerate((ag_hbm, ap_hbm, bg_hbm, bp_hbm))]
    small += [pltpu.make_async_copy(ref, vector_ref.at[pl.ds(n, 1)], sem.at[4 + n]) for n, ref in enumerate((gain_hbm, bias_hbm))]
    start(small)
    fetch = pltpu.make_async_copy(pair_hbm, pair_ref, sem.at[6])
    fetch.start()
    wait(small)
    weights = jnp.concatenate([weight_ref[n].T * jnp.asarray(0.5, BF16) for n in range(4)], axis=0)
    gain, bias = (jnp.concatenate([column(vector_ref[n : n + 1], LANES)] * half, axis=1) for n in range(2))
    fetch.wait()
    block = jnp.concatenate([pair_ref[row] for s in range(half) for row in (s, half + s)], axis=0)
    centered = dot(centring(chans), block, (1, 1))
    variance = jnp.mean(centered * centered, axis=0, keepdims=True)
    normed = (centered * lax.rsqrt(variance + EPS) * gain + bias).astype(BF16)
    projected = dot(weights, normed, (1, 0))
    a_gate, a_proj, b_gate, b_proj = (projected[n * chans : (n + 1) * chans] for n in range(4))
    left, right = a_proj + jnp.tanh(a_gate) * a_proj, b_proj + jnp.tanh(b_gate) * b_proj
    pitch = 2 * half + 1
    for s in range(half):
        cut = slice(s * LANES, (s + 1) * LANES)
        wide_ref[pl.ds(s, chans, stride=pitch), :] = left[:, cut]
        wide_ref[pl.ds(half + s, chans, stride=pitch), :] = right[:, cut]
    for c in range(chans):
        out_ref[c] = wide_ref[pl.ds(c * pitch, 2 * half), :].astype(BF16)


def gate_kernel(
    pair_hbm, gain_hbm, bias_hbm, weight_hbm, mid_gain_hbm, mid_bias_hbm, out_proj_hbm,
    out_ref, mid_gain_ref, mid_bias_ref, out_proj_ref, pair_ref, vector_ref, weight_ref, sem,
):
    rows, cols, chans = pair_hbm.shape
    copies = [
        pltpu.make_async_copy(pair_hbm, pair_ref, sem.at[0]),
        pltpu.make_async_copy(weight_hbm, weight_ref, sem.at[1]),
        pltpu.make_async_copy(out_proj_hbm, out_proj_ref, sem.at[2]),
    ]
    vectors = (gain_hbm, bias_hbm, mid_gain_hbm, mid_bias_hbm)
    copies += [pltpu.make_async_copy(ref, vector_ref.at[pl.ds(n, 1)], sem.at[3 + n]) for n, ref in enumerate(vectors)]
    wait(start(copies))
    mid_gain_ref[...] = column(vector_ref[2:3], LANES)
    mid_bias_ref[...] = column(vector_ref[3:4], LANES)
    values = pair_ref[...].reshape(rows * cols, chans).astype(F32)
    normed = (norm(values, 1) * vector_ref[0:1] + vector_ref[1:2]).astype(BF16)
    out_ref[...] = sigmoid(dot(normed, weight_ref[...], (1, 0))).reshape(out_ref.shape)


def merge(even, odd, cols):
    return [jnp.concatenate([even[:, cut], odd[:, cut]], axis=1) for cut in (slice(0, cols), slice(cols, 2 * cols))]


def product_kernel(in_ref, out_ref):
    row_count, col_count, tiles, lanes = in_ref.shape
    tile, cols, depth = tiles // 2, lanes // 2, col_count * lanes // 2
    count = row_count * tile
    pairs = range(col_count // 2)

    def operand(part):
        parts = [
            merge(*(in_ref[:, 2 * m + odd, part, :].reshape(count, lanes) for odd in range(2)), cols) for m in pairs
        ]
        return [jnp.concatenate([part[h] for part in parts], axis=1) for h in range(2)]

    left, right = operand(pl.ds(0, tile)), operand(pl.ds(tile, tile))
    right = jnp.stack([half.reshape(row_count, tile, depth) for half in right], axis=1).reshape(2 * count, depth)
    products = [dot(half, right, (1, 1)).astype(BF16) for half in left]
    for m in pairs:
        cut = slice(m * lanes, (m + 1) * lanes)
        for odd, block in enumerate(merge(*(half[:, cut] for half in products), cols)):
            out_ref[:, 2 * m + odd] = block.reshape(row_count, tile, lanes)


def update_kernel(in_ref, gate_ref, gain_ref, bias_ref, weight_ref, out_hbm, wide_ref, out_ref, sem):
    chans, half, lanes = in_ref.shape
    cols = lanes // 2
    pitch = half + 1
    normed = norm(in_ref[...].astype(F32), 0)
    for c in range(chans):
        wide_ref[pl.ds(c * pitch, half), :] = normed[c]
    step = half // PARTS
    copies = []
    for s in range(half):
        mixed = (wide_ref[pl.ds(s, chans, stride=pitch), :] * gain_ref[...] + bias_ref[...]).astype(BF16)
        output = dot(mixed, weight_ref[...], (0, 0))
        out_ref[s] = (gate_ref[s] * output[:cols]).astype(BF16)
        out_ref[half + s] = (gate_ref[half + s] * output[cols:]).astype(BF16)
        if s % step == step - 1:
            for h in range(2):
                at = pl.ds(h * half + s - step + 1, step)
                copies += start([pltpu.make_async_copy(out_ref.at[at], out_hbm.at[at], sem.at[len(copies)])])
    wait(copies)


LANES = 128
PARTS = 4
VMEM_LIMIT = 48 * 2**20


def in_hbm(*arrays):
    return [pltpu.with_memory_space_constraint(array, pltpu.HBM) for array in arrays]


def call(kernel, out, scratch=(), flops=0, **specs):
    return pl.pallas_call(
        kernel,
        out_shape=out,
        scratch_shapes=list(scratch),
        compiler_params=pltpu.CompilerParams(vmem_limit_bytes=VMEM_LIMIT),
        cost_estimate=pl.CostEstimate(flops=flops, bytes_accessed=2**20, transcendentals=2**18),
        **specs,
    )


def per_device(
    pair, in_gain, in_bias, a_gate, a_proj, b_gate, b_proj, out_gate, mid_gain, mid_bias, out_proj
):
    rows, cols, chans = pair.shape
    hidden = a_gate.shape[1]
    row_count, col_count = lax.axis_size("row"), lax.axis_size("col")
    half, lanes = rows // 2, 2 * cols
    hbm = pl.BlockSpec(memory_space=pltpu.HBM)
    gain, bias = in_gain[None, :], in_bias[None, :]
    operands = call(
        operands_kernel,
        jax.ShapeDtypeStruct((hidden, 2 * half, lanes), BF16),
        [
            pltpu.VMEM(pair.shape, BF16),
            pltpu.VMEM((8, chans), F32),
            pltpu.VMEM((4, chans, hidden), BF16),
            pltpu.VMEM(((hidden + 8) * (2 * half + 1), lanes), F32),
            pltpu.SemaphoreType.DMA((7,)),
        ],
        2 * rows * cols * chans * 4 * hidden,
        in_specs=[hbm] * 7,
    )(*in_hbm(pair, gain, bias, a_gate, a_proj, b_gate, b_proj))
    channel = lax.all_to_all(operands, BOTH, 0, 0, tiled=True)
    gate, mid_gain, mid_bias, out_proj = call(
        gate_kernel,
        (
            jax.ShapeDtypeStruct(pair.shape, F32),
            jax.ShapeDtypeStruct((hidden, lanes), F32),
            jax.ShapeDtypeStruct((hidden, lanes), F32),
            jax.ShapeDtypeStruct(out_proj.shape, BF16),
        ),
        [
            pltpu.VMEM(pair.shape, BF16),
            pltpu.VMEM((8, chans), F32),
            pltpu.VMEM(out_gate.shape, BF16),
            pltpu.SemaphoreType.DMA((7,)),
        ],
        2 * rows * cols * chans * chans,
        in_specs=[hbm] * 7,
    )(*in_hbm(pair, gain, bias, out_gate, mid_gain[None, :], mid_bias[None, :], out_proj))
    count, depth = row_count * half, col_count * cols
    triangle = call(
        product_kernel,
        jax.ShapeDtypeStruct((row_count, col_count, half, lanes), BF16),
        (),
        8 * count * count * depth,
    )(channel.reshape(row_count, col_count, 2 * half, lanes))
    triangle = lax.all_to_all(triangle.reshape(hidden, half, lanes), BOTH, 0, 0, tiled=True)
    return call(
        update_kernel,
        jax.ShapeDtypeStruct(pair.shape, BF16),
        [
            pltpu.VMEM(((hidden + 8) * (half + 1), lanes), F32),
            pltpu.VMEM(pair.shape, BF16),
            pltpu.SemaphoreType.DMA((2 * PARTS,)),
        ],
        2 * rows * cols * hidden * chans,
        out_specs=hbm,
    )(triangle, gate, mid_gain, mid_bias, out_proj)


def solution(mesh):
    in_specs = (P("row", "col", None), P(), P(), P(), P(), P(), P(), P(), P(), P(), P())
    return jax.shard_map(
        per_device, mesh=mesh, in_specs=in_specs, out_specs=P("row", "col", None), check_vma=False
    )
```

```python
import jax
import jax.numpy as jnp
from jax import lax
from jax.experimental import pallas as pl
from jax.experimental.pallas import tpu as pltpu
from jax.sharding import PartitionSpec as P

BF16, F32 = jnp.bfloat16, jnp.float32
EPS = 1e-05
BOTH = ("row", "col")


def sigmoid(x):
    return 0.5 + 0.5 * jnp.tanh(0.5 * x)


def centring(size):
    same = lax.broadcasted_iota(jnp.int32, (size, size), 0) == lax.broadcasted_iota(jnp.int32, (size, size), 1)
    return jnp.where(same, 1 - 1 / size, -1 / size).astype(BF16)


def dot(a, b, contract):
    return lax.dot_general(a, b, ((contract[:1], contract[1:]), ((), ())), preferred_element_type=F32)


def column(vector, width):
    return jnp.broadcast_to(vector, (width, vector.shape[1])).T


def norm(values, axis):
    mean = jnp.mean(values, axis=axis, keepdims=True)
    centered = values - mean
    variance = jnp.mean(centered * centered, axis=axis, keepdims=True)
    return centered * lax.rsqrt(variance + EPS)


def start(copies):
    for copy in copies:
        copy.start()
    return copies


def wait(copies):
    for copy in copies:
        copy.wait()


def operands_kernel(
    pair_hbm, gain_hbm, bias_hbm, ag_hbm, ap_hbm, bg_hbm, bp_hbm, gate_hbm, mid_gain_hbm, mid_bias_hbm, proj_hbm,
    out_ref, normed_ref, mid_gain_ref, mid_bias_ref, late_ref, pair_ref, vector_ref, weight_ref, wide_ref, sem,
):
    rows, _, chans = pair_hbm.shape
    half = rows // 2
    weights = (ag_hbm, ap_hbm, bg_hbm, bp_hbm, gate_hbm, proj_hbm)
    vectors = (gain_hbm, bias_hbm, mid_gain_hbm, mid_bias_hbm)
    small = [pltpu.make_async_copy(ref, weight_ref.at[n], sem.at[n]) for n, ref in enumerate(weights)]
    small += [
        pltpu.make_async_copy(ref, vector_ref.at[pl.ds(n, 1)], sem.at[len(weights) + n]) for n, ref in enumerate(vectors)
    ]
    start(small)
    fetch = pltpu.make_async_copy(pair_hbm, pair_ref, sem.at[len(small)])
    fetch.start()
    wait(small)
    weights = jnp.concatenate([weight_ref[n].T * jnp.asarray(0.5, BF16) for n in range(4)], axis=0)
    gain, bias = (jnp.concatenate([column(vector_ref[n : n + 1], LANES)] * half, axis=1) for n in range(2))
    mid_gain_ref[...], mid_bias_ref[...] = (column(vector_ref[n : n + 1], LANES) for n in (2, 3))
    late_ref[...] = weight_ref[pl.ds(4, 2)] * jnp.asarray(0.5, BF16)
    fetch.wait()
    block = jnp.concatenate([pair_ref[row] for s in range(half) for row in (s, half + s)], axis=0)
    centered = dot(centring(chans), block, (1, 1))
    variance = jnp.mean(centered * centered, axis=0, keepdims=True)
    normed = (centered * lax.rsqrt(variance + EPS) * gain + bias).astype(BF16)
    normed_ref[...] = normed
    projected = dot(weights, normed, (1, 0))
    a_gate, a_proj, b_gate, b_proj = (projected[n * chans : (n + 1) * chans] for n in range(4))
    left, right = a_proj + jnp.tanh(a_gate) * a_proj, b_proj + jnp.tanh(b_gate) * b_proj
    pitch = 2 * half + 1
    for s in range(half):
        cut = slice(s * LANES, (s + 1) * LANES)
        wide_ref[pl.ds(s, chans, stride=pitch), :] = left[:, cut]
        wide_ref[pl.ds(half + s, chans, stride=pitch), :] = right[:, cut]
    for c in range(chans):
        out_ref[c] = wide_ref[pl.ds(c * pitch, 2 * half), :].astype(BF16)


def merge(even, odd, cols):
    return [jnp.concatenate([even[:, cut], odd[:, cut]], axis=1) for cut in (slice(0, cols), slice(cols, 2 * cols))]


def product_kernel(in_ref, out_ref):
    row_count, col_count, tiles, lanes = in_ref.shape
    tile, cols, depth = tiles // 2, lanes // 2, col_count * lanes // 2
    count = row_count * tile
    pairs = range(col_count // 2)

    def operand(part):
        parts = [
            merge(*(in_ref[:, 2 * m + odd, part, :].reshape(count, lanes) for odd in range(2)), cols) for m in pairs
        ]
        return [jnp.concatenate([part[h] for part in parts], axis=1) for h in range(2)]

    left, right = operand(pl.ds(0, tile)), operand(pl.ds(tile, tile))
    right = jnp.stack([half.reshape(row_count, tile, depth) for half in right], axis=1).reshape(2 * count, depth)
    product = dot(jnp.concatenate(left, axis=0), right, (1, 1)).astype(BF16)
    products = [product[:count], product[count:]]
    for m in pairs:
        cut = slice(m * lanes, (m + 1) * lanes)
        for odd, block in enumerate(merge(*(half[:, cut] for half in products), cols)):
            out_ref[:, 2 * m + odd] = block.reshape(row_count, tile, lanes)


def update_kernel(in_ref, normed_ref, gain_ref, bias_ref, weight_ref, out_hbm, wide_ref, out_ref, sem):
    chans, half, lanes = in_ref.shape
    cols = lanes // 2
    pitch = half + 1
    normed = norm(in_ref[...].astype(F32), 0)
    for c in range(chans):
        wide_ref[pl.ds(c * pitch, half), :] = normed[c]
    step = half // PARTS
    copies = []
    for s in range(half):
        mixed = (wide_ref[pl.ds(s, chans, stride=pitch), :] * gain_ref[...] + bias_ref[...]).astype(BF16)
        output = dot(mixed, weight_ref[1], (0, 0))
        gate = jnp.tanh(dot(normed_ref[:, s * lanes : (s + 1) * lanes], weight_ref[0], (0, 0)))
        update = (output + gate * output).astype(BF16)
        out_ref[s], out_ref[half + s] = update[:cols], update[cols:]
        if s % step == step - 1:
            for h in range(2):
                at = pl.ds(h * half + s - step + 1, step)
                copies += start([pltpu.make_async_copy(out_ref.at[at], out_hbm.at[at], sem.at[len(copies)])])
    wait(copies)


LANES = 128
PARTS = 4
VMEM_LIMIT = 48 * 2**20


def in_hbm(*arrays):
    return [pltpu.with_memory_space_constraint(array, pltpu.HBM) for array in arrays]


def call(kernel, out, scratch=(), flops=0, **specs):
    return pl.pallas_call(
        kernel,
        out_shape=out,
        scratch_shapes=list(scratch),
        compiler_params=pltpu.CompilerParams(vmem_limit_bytes=VMEM_LIMIT),
        cost_estimate=pl.CostEstimate(flops=flops, bytes_accessed=2**20, transcendentals=2**18),
        **specs,
    )


def per_device(
    pair, in_gain, in_bias, a_gate, a_proj, b_gate, b_proj, out_gate, mid_gain, mid_bias, out_proj
):
    rows, cols, chans = pair.shape
    hidden = a_gate.shape[1]
    row_count, col_count = lax.axis_size("row"), lax.axis_size("col")
    half, lanes = rows // 2, 2 * cols
    hbm = pl.BlockSpec(memory_space=pltpu.HBM)
    late = jax.ShapeDtypeStruct((hidden, lanes), F32)
    operands, normed, mid_gain, mid_bias, weights = call(
        operands_kernel,
        (
            jax.ShapeDtypeStruct((hidden, 2 * half, lanes), BF16),
            jax.ShapeDtypeStruct((chans, rows * cols), BF16),
            late,
            late,
            jax.ShapeDtypeStruct((2, chans, hidden), BF16),
        ),
        [
            pltpu.VMEM(pair.shape, BF16),
            pltpu.VMEM((8, chans), F32),
            pltpu.VMEM((6, chans, hidden), BF16),
            pltpu.VMEM(((hidden + 8) * (2 * half + 1), lanes), F32),
            pltpu.SemaphoreType.DMA((11,)),
        ],
        2 * rows * cols * chans * 4 * hidden,
        in_specs=[hbm] * 11,
    )(
        *in_hbm(
            pair, in_gain[None, :], in_bias[None, :], a_gate, a_proj, b_gate, b_proj,
            out_gate, mid_gain[None, :], mid_bias[None, :], out_proj,
        )
    )
    channel = lax.all_to_all(operands, BOTH, 0, 0, tiled=True)
    count, depth = row_count * half, col_count * cols
    triangle = call(
        product_kernel,
        jax.ShapeDtypeStruct((row_count, col_count, half, lanes), BF16),
        (),
        8 * count * count * depth,
    )(channel.reshape(row_count, col_count, 2 * half, lanes))
    triangle = lax.all_to_all(triangle.reshape(hidden, half, lanes), BOTH, 0, 0, tiled=True)
    return call(
        update_kernel,
        jax.ShapeDtypeStruct(pair.shape, BF16),
        [
            pltpu.VMEM(((hidden + 8) * (half + 1), lanes), F32),
            pltpu.VMEM(pair.shape, BF16),
            pltpu.SemaphoreType.DMA((2 * PARTS,)),
        ],
        2 * rows * cols * hidden * chans,
        out_specs=hbm,
    )(triangle, normed, mid_gain, mid_bias, weights)


def solution(mesh):
    in_specs = (P("row", "col", None), P(), P(), P(), P(), P(), P(), P(), P(), P(), P())
    return jax.shard_map(
        per_device, mesh=mesh, in_specs=in_specs, out_specs=P("row", "col", None), check_vma=False
    )
```

```python
import functools

import jax
import jax.numpy as jnp
from jax import lax
from jax.experimental import pallas as pl
from jax.experimental.pallas import tpu as pltpu
from jax.sharding import PartitionSpec as P

BF16, F32 = jnp.bfloat16, jnp.float32
EPS = 1e-05
BOTH = ("row", "col")
FIRST = (6, 2)


def chips(row_count, col_count):
    first = FIRST[0] * col_count + FIRST[1]
    return [first] + [n for n in range(row_count // 2 * col_count) if n != first]


def exchange(values, row_count, col_count):
    devices = [
        [(2 * (n // col_count) + core) * col_count + n % col_count for n in chips(row_count, col_count)]
        for core in range(2)
    ]
    return lax.all_to_all(values, BOTH, 0, 0, axis_index_groups=devices, tiled=True)


def sigmoid(x):
    return 0.5 + 0.5 * jnp.tanh(0.5 * x)


def centring(size):
    same = lax.broadcasted_iota(jnp.int32, (size, size), 0) == lax.broadcasted_iota(jnp.int32, (size, size), 1)
    return jnp.where(same, 1 - 1 / size, -1 / size).astype(BF16)


def dot(a, b, contract):
    return lax.dot_general(a, b, ((contract[:1], contract[1:]), ((), ())), preferred_element_type=F32)


def column(vector, width):
    return jnp.broadcast_to(vector, (width, vector.shape[1])).T


def norm(values, axis):
    mean = jnp.mean(values, axis=axis, keepdims=True)
    centered = values - mean
    variance = jnp.mean(centered * centered, axis=axis, keepdims=True)
    return centered * lax.rsqrt(variance + EPS)


def start(copies):
    for copy in copies:
        copy.start()
    return copies


def wait(copies):
    for copy in copies:
        copy.wait()


def operands_kernel(
    pair_hbm, gain_hbm, bias_hbm, ag_hbm, ap_hbm, bg_hbm, bp_hbm, gate_hbm, mid_gain_hbm, mid_bias_hbm, proj_hbm,
    out_ref, normed_ref, mid_gain_ref, mid_bias_ref, late_ref, pair_ref, vector_ref, weight_ref, wide_ref, sem,
):
    rows, _, chans = pair_hbm.shape
    half = rows // 2
    weights = (ag_hbm, ap_hbm, bg_hbm, bp_hbm, gate_hbm, proj_hbm)
    vectors = (gain_hbm, bias_hbm, mid_gain_hbm, mid_bias_hbm)
    small = [pltpu.make_async_copy(ref, weight_ref.at[n], sem.at[n]) for n, ref in enumerate(weights)]
    small += [
        pltpu.make_async_copy(ref, vector_ref.at[pl.ds(n, 1)], sem.at[len(weights) + n]) for n, ref in enumerate(vectors)
    ]
    start(small)
    fetch = pltpu.make_async_copy(pair_hbm, pair_ref, sem.at[len(small)])
    fetch.start()
    wait(small)
    weights = jnp.concatenate([weight_ref[n].T * jnp.asarray(0.5, BF16) for n in range(4)], axis=0)
    gain, bias = (jnp.concatenate([column(vector_ref[n : n + 1], LANES)] * half, axis=1) for n in range(2))
    mid_gain_ref[...], mid_bias_ref[...] = (column(vector_ref[n : n + 1], LANES) for n in (2, 3))
    late_ref[...] = weight_ref[pl.ds(4, 2)] * jnp.asarray(0.5, BF16)
    fetch.wait()
    block = jnp.concatenate([pair_ref[row] for s in range(half) for row in (s, half + s)], axis=0)
    centered = dot(centring(chans), block, (1, 1))
    variance = jnp.mean(centered * centered, axis=0, keepdims=True)
    normed = (centered * lax.rsqrt(variance + EPS) * gain + bias).astype(BF16)
    normed_ref[...] = normed
    projected = dot(weights, normed, (1, 0))
    a_gate, a_proj, b_gate, b_proj = (projected[n * chans : (n + 1) * chans] for n in range(4))
    left, right = a_proj + jnp.tanh(a_gate) * a_proj, b_proj + jnp.tanh(b_gate) * b_proj
    pitch = 2 * half + 1
    for s in range(half):
        cut = slice(s * LANES, (s + 1) * LANES)
        wide_ref[pl.ds(s, chans, stride=pitch), :] = left[:, cut]
        wide_ref[pl.ds(half + s, chans, stride=pitch), :] = right[:, cut]
    for c in range(chans):
        out_ref[c] = wide_ref[pl.ds(c * pitch, 2 * half), :].astype(BF16)


def merge(even, odd, cols):
    return [jnp.concatenate([even[:, cut], odd[:, cut]], axis=1) for cut in (slice(0, cols), slice(cols, 2 * cols))]


def arrange_kernel(order, part, in_ref, out_ref):
    channels, rows, _, tile, depth = out_ref.shape
    lanes = in_ref.shape[3]
    count = 2 * depth // lanes
    for channel in range(channels):
        for row in range(rows):
            tiles = [in_ref[order.index(row * count + col), channel, pl.ds(part * tile, tile), :] for col in range(count)]
            for m in range(count // 2):
                for h, block in enumerate(merge(tiles[2 * m], tiles[2 * m + 1], lanes // 2)):
                    out_ref[channel, row, h, :, m * lanes : (m + 1) * lanes] = block


def product_kernel(order, left_ref, right_ref, other_ref, out_ref):
    channels, rows, _, tile, depth = left_ref.shape
    lanes = out_ref.shape[3]
    cols, count = lanes // 2, rows * tile
    core = lax.rem(lax.axis_index("row"), 2)
    for channel in range(channels):
        own, other = right_ref[channel], other_ref[channel]
        right = jnp.stack([jnp.where(core == 0, own, other), jnp.where(core == 0, other, own)], axis=1)
        right = right.reshape(4 * count, depth)
        left = jnp.concatenate([left_ref[channel, :, h].reshape(count, depth) for h in range(2)], axis=0)
        product = dot(left, right, (1, 1)).astype(BF16)
        for m in range(4 * count // lanes):
            cut = slice(m * lanes, (m + 1) * lanes)
            for odd, block in enumerate(merge(product[:count, cut], product[count:, cut], cols)):
                for row in range(rows):
                    at = order.index(row * (4 * count // cols) + 2 * m + odd)
                    out_ref[at, channel] = block[row * tile : (row + 1) * tile]


def update_kernel(in_ref, normed_ref, gain_ref, bias_ref, weight_ref, out_hbm, wide_ref, out_ref, sem):
    chans, half, lanes = in_ref.shape
    cols = lanes // 2
    pitch = half + 1
    normed = norm(in_ref[...].astype(F32), 0)
    for c in range(chans):
        wide_ref[pl.ds(c * pitch, half), :] = normed[c]
    step = half // PARTS
    copies = []
    for s in range(half):
        mixed = (wide_ref[pl.ds(s, chans, stride=pitch), :] * gain_ref[...] + bias_ref[...]).astype(BF16)
        output = dot(mixed, weight_ref[1], (0, 0))
        gate = jnp.tanh(dot(normed_ref[:, s * lanes : (s + 1) * lanes], weight_ref[0], (0, 0)))
        update = (output + gate * output).astype(BF16)
        out_ref[s], out_ref[half + s] = update[:cols], update[cols:]
        if s % step == step - 1:
            for h in range(2):
                at = pl.ds(h * half + s - step + 1, step)
                copies += start([pltpu.make_async_copy(out_ref.at[at], out_hbm.at[at], sem.at[len(copies)])])
    wait(copies)


LANES = 128
PARTS = 4
VMEM_LIMIT = 48 * 2**20


def in_hbm(*arrays):
    return [pltpu.with_memory_space_constraint(array, pltpu.HBM) for array in arrays]


def call(kernel, out, scratch=(), flops=0, **specs):
    return pl.pallas_call(
        kernel,
        out_shape=out,
        scratch_shapes=list(scratch),
        compiler_params=pltpu.CompilerParams(vmem_limit_bytes=VMEM_LIMIT),
        cost_estimate=pl.CostEstimate(flops=flops, bytes_accessed=2**20, transcendentals=2**18),
        **specs,
    )


def per_device(
    pair, in_gain, in_bias, a_gate, a_proj, b_gate, b_proj, out_gate, mid_gain, mid_bias, out_proj
):
    rows, cols, chans = pair.shape
    hidden = a_gate.shape[1]
    row_count, col_count = lax.axis_size("row"), lax.axis_size("col")
    half, lanes = rows // 2, 2 * cols
    hbm = pl.BlockSpec(memory_space=pltpu.HBM)
    late = jax.ShapeDtypeStruct((hidden, lanes), F32)
    operands, normed, mid_gain, mid_bias, weights = call(
        operands_kernel,
        (
            jax.ShapeDtypeStruct((hidden, 2 * half, lanes), BF16),
            jax.ShapeDtypeStruct((chans, rows * cols), BF16),
            late,
            late,
            jax.ShapeDtypeStruct((2, chans, hidden), BF16),
        ),
        [
            pltpu.VMEM(pair.shape, BF16),
            pltpu.VMEM((8, chans), F32),
            pltpu.VMEM((6, chans, hidden), BF16),
            pltpu.VMEM(((hidden + 8) * (2 * half + 1), lanes), F32),
            pltpu.SemaphoreType.DMA((11,)),
        ],
        2 * rows * cols * chans * 4 * hidden,
        in_specs=[hbm] * 11,
    )(
        *in_hbm(
            pair, in_gain[None, :], in_bias[None, :], a_gate, a_proj, b_gate, b_proj,
            out_gate, mid_gain[None, :], mid_bias[None, :], out_proj,
        )
    )
    order = chips(row_count, col_count)
    count, depth = row_count // 2, col_count * cols
    messages = exchange(operands.reshape(len(order), 4 * half, lanes), row_count, col_count)
    messages = messages.reshape(len(order), 2, 2 * half, lanes)
    arranged = jax.ShapeDtypeStruct((2, count, 2, half, depth), BF16)
    left, right = (
        call(functools.partial(arrange_kernel, order, part), arranged)(messages) for part in range(2)
    )
    other = lax.ppermute(right, "row", [(row, row ^ 1) for row in range(row_count)])
    triangle = call(
        functools.partial(product_kernel, order),
        jax.ShapeDtypeStruct((len(order), 2, half, lanes), BF16),
        (),
        2 * 2 * (2 * count * half) * (4 * count * half) * depth,
    )(left, right, other)
    triangle = exchange(triangle.reshape(len(order), 2 * half, lanes), row_count, col_count)
    triangle = triangle.reshape(hidden, half, lanes)
    return call(
        update_kernel,
        jax.ShapeDtypeStruct(pair.shape, BF16),
        [
            pltpu.VMEM(((hidden + 8) * (half + 1), lanes), F32),
            pltpu.VMEM(pair.shape, BF16),
            pltpu.SemaphoreType.DMA((2 * PARTS,)),
        ],
        2 * rows * cols * hidden * chans,
        out_specs=hbm,
    )(triangle, normed, mid_gain, mid_bias, weights)


def solution(mesh):
    in_specs = (P("row", "col", None), P(), P(), P(), P(), P(), P(), P(), P(), P(), P())
    return jax.shard_map(
        per_device, mesh=mesh, in_specs=in_specs, out_specs=P("row", "col", None), check_vma=False
    )
```

```python
import functools

import jax
import jax.numpy as jnp
from jax import lax
from jax.experimental import pallas as pl
from jax.experimental.pallas import tpu as pltpu
from jax.sharding import PartitionSpec as P

BF16, F32 = jnp.bfloat16, jnp.float32
EPS = 1e-05
BOTH = ("row", "col")
FIRST = (6, 2)


def chips(row_count, col_count):
    first = FIRST[0] * col_count + FIRST[1]
    return [first] + [n for n in range(row_count // 2 * col_count) if n != first]


def exchange(values, row_count, col_count):
    devices = [
        [(2 * (n // col_count) + core) * col_count + n % col_count for n in chips(row_count, col_count)]
        for core in range(2)
    ]
    return lax.all_to_all(values, BOTH, 0, 0, axis_index_groups=devices, tiled=True)


def sigmoid(x):
    return 0.5 + 0.5 * jnp.tanh(0.5 * x)


def centring(size):
    same = lax.broadcasted_iota(jnp.int32, (size, size), 0) == lax.broadcasted_iota(jnp.int32, (size, size), 1)
    return jnp.where(same, 1 - 1 / size, -1 / size).astype(BF16)


def dot(a, b, contract):
    return lax.dot_general(a, b, ((contract[:1], contract[1:]), ((), ())), preferred_element_type=F32)


def column(vector, width):
    return jnp.broadcast_to(vector, (width, vector.shape[1])).T


def norm(values, axis):
    mean = jnp.mean(values, axis=axis, keepdims=True)
    centered = values - mean
    variance = jnp.mean(centered * centered, axis=axis, keepdims=True)
    return centered * lax.rsqrt(variance + EPS)


def start(copies):
    for copy in copies:
        copy.start()
    return copies


def wait(copies):
    for copy in copies:
        copy.wait()


def operands_kernel(
    pair_hbm, gain_hbm, bias_hbm, ag_hbm, ap_hbm, bg_hbm, bp_hbm, gate_hbm, mid_gain_hbm, mid_bias_hbm, proj_hbm,
    out_ref, normed_ref, mid_gain_ref, mid_bias_ref, late_ref, pair_ref, vector_ref, weight_ref, wide_ref, sem,
):
    rows, _, chans = pair_hbm.shape
    half = rows // 2
    weights = (ag_hbm, ap_hbm, bg_hbm, bp_hbm, gate_hbm, proj_hbm)
    vectors = (gain_hbm, bias_hbm, mid_gain_hbm, mid_bias_hbm)
    small = [pltpu.make_async_copy(ref, weight_ref.at[n], sem.at[n]) for n, ref in enumerate(weights)]
    small += [
        pltpu.make_async_copy(ref, vector_ref.at[pl.ds(n, 1)], sem.at[len(weights) + n]) for n, ref in enumerate(vectors)
    ]
    fetch = pltpu.make_async_copy(pair_hbm, pair_ref, sem.at[len(small)])
    fetch.start()
    start(small)
    wait(small)
    weights = jnp.concatenate([weight_ref[n].T * jnp.asarray(0.5, BF16) for n in range(4)], axis=0)
    gain, bias = (jnp.concatenate([column(vector_ref[n : n + 1], LANES)] * half, axis=1) for n in range(2))
    mid_gain_ref[...], mid_bias_ref[...] = (column(vector_ref[n : n + 1], LANES) for n in (2, 3))
    late_ref[...] = weight_ref[pl.ds(4, 2)] * jnp.asarray(0.5, BF16)
    fetch.wait()
    block = jnp.concatenate([pair_ref[row] for s in range(half) for row in (s, half + s)], axis=0)
    centered = dot(centring(chans), block, (1, 1))
    variance = jnp.mean(centered * centered, axis=0, keepdims=True)
    normed = (centered * lax.rsqrt(variance + EPS) * gain + bias).astype(BF16)
    normed_ref[...] = normed
    projected = dot(weights, normed, (1, 0))
    a_gate, a_proj, b_gate, b_proj = (projected[n * chans : (n + 1) * chans] for n in range(4))
    left, right = a_proj + jnp.tanh(a_gate) * a_proj, b_proj + jnp.tanh(b_gate) * b_proj
    pitch = 2 * half + 1
    for s in range(half):
        cut = slice(s * LANES, (s + 1) * LANES)
        wide_ref[pl.ds(s, chans, stride=pitch), :] = left[:, cut]
        wide_ref[pl.ds(half + s, chans, stride=pitch), :] = right[:, cut]
    for c in range(chans):
        out_ref[c] = wide_ref[pl.ds(c * pitch, 2 * half), :].astype(BF16)


def merge(even, odd, cols):
    return [jnp.concatenate([even[:, cut], odd[:, cut]], axis=1) for cut in (slice(0, cols), slice(cols, 2 * cols))]


def arrange_kernel(order, part, in_ref, out_ref):
    channels, rows, _, tile, depth = out_ref.shape
    lanes = in_ref.shape[3]
    count = 2 * depth // lanes
    for channel in range(channels):
        for row in range(rows):
            tiles = [in_ref[order.index(row * count + col), channel, pl.ds(part * tile, tile), :] for col in range(count)]
            for m in range(count // 2):
                for h, block in enumerate(merge(tiles[2 * m], tiles[2 * m + 1], lanes // 2)):
                    out_ref[channel, row, h, :, m * lanes : (m + 1) * lanes] = block


def gate_kernel(order, in_ref, normed_ref, weight_ref, out_ref, gate_ref):
    arrange_kernel(order, 0, in_ref, out_ref)
    half, lanes, _ = gate_ref.shape
    for s in range(half):
        gate_ref[s] = 1 + jnp.tanh(dot(normed_ref[:, s * lanes : (s + 1) * lanes], weight_ref[0], (0, 0)))


def product_kernel(order, left_ref, right_ref, other_ref, out_ref):
    channels, rows, _, tile, depth = left_ref.shape
    lanes = out_ref.shape[3]
    cols, count = lanes // 2, rows * tile
    core = lax.rem(lax.axis_index("row"), 2)
    for channel in range(channels):
        own, other = right_ref[channel], other_ref[channel]
        right = jnp.stack([jnp.where(core == 0, own, other), jnp.where(core == 0, other, own)], axis=1)
        right = right.reshape(4 * count, depth)
        left = jnp.concatenate([left_ref[channel, :, h].reshape(count, depth) for h in range(2)], axis=0)
        product = dot(left, right, (1, 1)).astype(BF16)
        for m in range(4 * count // lanes):
            cut = slice(m * lanes, (m + 1) * lanes)
            for odd, block in enumerate(merge(product[:count, cut], product[count:, cut], cols)):
                for row in range(rows):
                    at = order.index(row * (4 * count // cols) + 2 * m + odd)
                    out_ref[at, channel] = block[row * tile : (row + 1) * tile]


def update_kernel(in_ref, gate_ref, gain_ref, bias_ref, weight_ref, out_hbm, wide_ref, out_ref, sem):
    chans, half, lanes = in_ref.shape
    cols = lanes // 2
    pitch = half + 1
    normed = norm(in_ref[...].astype(F32), 0)
    for c in range(chans):
        wide_ref[pl.ds(c * pitch, half), :] = normed[c]
    step = half // PARTS
    copies = []
    for s in range(half):
        mixed = (wide_ref[pl.ds(s, chans, stride=pitch), :] * gain_ref[...] + bias_ref[...]).astype(BF16)
        output = dot(mixed, weight_ref[1], (0, 0))
        update = (gate_ref[s] * output).astype(BF16)
        out_ref[s], out_ref[half + s] = update[:cols], update[cols:]
        if s % step == step - 1:
            for h in range(2):
                at = pl.ds(h * half + s - step + 1, step)
                copies += start([pltpu.make_async_copy(out_ref.at[at], out_hbm.at[at], sem.at[len(copies)])])
    wait(copies)


LANES = 128
PARTS = 4
VMEM_LIMIT = 48 * 2**20


def in_hbm(*arrays):
    return [pltpu.with_memory_space_constraint(array, pltpu.HBM) for array in arrays]


def call(kernel, out, scratch=(), flops=0, **specs):
    return pl.pallas_call(
        kernel,
        out_shape=out,
        scratch_shapes=list(scratch),
        compiler_params=pltpu.CompilerParams(vmem_limit_bytes=VMEM_LIMIT),
        cost_estimate=pl.CostEstimate(flops=flops, bytes_accessed=2**20, transcendentals=2**18),
        **specs,
    )


def per_device(
    pair, in_gain, in_bias, a_gate, a_proj, b_gate, b_proj, out_gate, mid_gain, mid_bias, out_proj
):
    rows, cols, chans = pair.shape
    hidden = a_gate.shape[1]
    row_count, col_count = lax.axis_size("row"), lax.axis_size("col")
    half, lanes = rows // 2, 2 * cols
    hbm = pl.BlockSpec(memory_space=pltpu.HBM)
    late = jax.ShapeDtypeStruct((hidden, lanes), F32)
    operands, normed, mid_gain, mid_bias, weights = call(
        operands_kernel,
        (
            jax.ShapeDtypeStruct((hidden, 2 * half, lanes), BF16),
            jax.ShapeDtypeStruct((chans, rows * cols), BF16),
            late,
            late,
            jax.ShapeDtypeStruct((2, chans, hidden), BF16),
        ),
        [
            pltpu.VMEM(pair.shape, BF16),
            pltpu.VMEM((8, chans), F32),
            pltpu.VMEM((6, chans, hidden), BF16),
            pltpu.VMEM(((hidden + 8) * (2 * half + 1), lanes), F32),
            pltpu.SemaphoreType.DMA((11,)),
        ],
        2 * rows * cols * chans * 4 * hidden,
        in_specs=[hbm] * 11,
    )(
        *in_hbm(
            pair, in_gain[None, :], in_bias[None, :], a_gate, a_proj, b_gate, b_proj,
            out_gate, mid_gain[None, :], mid_bias[None, :], out_proj,
        )
    )
    order = chips(row_count, col_count)
    count, depth = row_count // 2, col_count * cols
    messages = exchange(operands.reshape(len(order), 4 * half, lanes), row_count, col_count)
    messages = messages.reshape(len(order), 2, 2 * half, lanes)
    arranged = jax.ShapeDtypeStruct((2, count, 2, half, depth), BF16)
    right = call(functools.partial(arrange_kernel, order, 1), arranged)(messages)
    other = lax.ppermute(right, "row", [(row, row ^ 1) for row in range(row_count)])
    left, gate = call(
        functools.partial(gate_kernel, order), (arranged, jax.ShapeDtypeStruct((half, lanes, chans), F32))
    )(messages, normed, weights)
    triangle = call(
        functools.partial(product_kernel, order),
        jax.ShapeDtypeStruct((len(order), 2, half, lanes), BF16),
        (),
        2 * 2 * (2 * count * half) * (4 * count * half) * depth,
    )(left, right, other)
    triangle = exchange(triangle.reshape(len(order), 2 * half, lanes), row_count, col_count)
    triangle = triangle.reshape(hidden, half, lanes)
    return call(
        update_kernel,
        jax.ShapeDtypeStruct(pair.shape, BF16),
        [
            pltpu.VMEM(((hidden + 8) * (half + 1), lanes), F32),
            pltpu.VMEM(pair.shape, BF16),
            pltpu.SemaphoreType.DMA((2 * PARTS,)),
        ],
        2 * rows * cols * hidden * chans,
        out_specs=hbm,
    )(triangle, gate, mid_gain, mid_bias, weights)


def solution(mesh):
    in_specs = (P("row", "col", None), P(), P(), P(), P(), P(), P(), P(), P(), P(), P())
    return jax.shard_map(
        per_device, mesh=mesh, in_specs=in_specs, out_specs=P("row", "col", None), check_vma=False
    )
```

```python
import functools

import jax
import jax.numpy as jnp
from jax import lax
from jax.experimental import pallas as pl
from jax.experimental.pallas import tpu as pltpu
from jax.sharding import PartitionSpec as P

BF16, F32 = jnp.bfloat16, jnp.float32
EPS = 1e-05
BOTH = ("row", "col")
FIRST = (6, 2)


def chips(row_count, col_count):
    first = FIRST[0] * col_count + FIRST[1]
    return [first] + [n for n in range(row_count // 2 * col_count) if n != first]


def exchange(values, row_count, col_count):
    devices = [
        [(2 * (n // col_count) + core) * col_count + n % col_count for n in chips(row_count, col_count)]
        for core in range(2)
    ]
    return lax.all_to_all(values, BOTH, 0, 0, axis_index_groups=devices, tiled=True)


def sigmoid(x):
    return 0.5 + 0.5 * jnp.tanh(0.5 * x)


def centring(size):
    same = lax.broadcasted_iota(jnp.int32, (size, size), 0) == lax.broadcasted_iota(jnp.int32, (size, size), 1)
    return jnp.where(same, 1 - 1 / size, -1 / size).astype(BF16)


def dot(a, b, contract):
    return lax.dot_general(a, b, ((contract[:1], contract[1:]), ((), ())), preferred_element_type=F32)


def column(vector, width):
    return jnp.broadcast_to(vector, (width, vector.shape[1])).T


def norm(values, axis):
    mean = jnp.mean(values, axis=axis, keepdims=True)
    centered = values - mean
    variance = jnp.mean(centered * centered, axis=axis, keepdims=True)
    return centered * lax.rsqrt(variance + EPS)


def start(copies):
    for copy in copies:
        copy.start()
    return copies


def wait(copies):
    for copy in copies:
        copy.wait()


def operands_kernel(
    pair_hbm, gain_hbm, bias_hbm, ag_hbm, ap_hbm, bg_hbm, bp_hbm,
    out_ref, normed_ref, pair_ref, vector_ref, weight_ref, wide_ref, sem,
):
    rows, _, chans = pair_hbm.shape
    half = rows // 2
    weights, vectors = (ag_hbm, ap_hbm, bg_hbm, bp_hbm), (gain_hbm, bias_hbm)
    small = [pltpu.make_async_copy(ref, weight_ref.at[n], sem.at[n]) for n, ref in enumerate(weights)]
    small += [
        pltpu.make_async_copy(ref, vector_ref.at[pl.ds(n, 1)], sem.at[len(weights) + n]) for n, ref in enumerate(vectors)
    ]
    fetch = pltpu.make_async_copy(pair_hbm, pair_ref, sem.at[len(small)])
    fetch.start()
    start(small)
    wait(small)
    weights = jnp.concatenate([weight_ref[n].T * jnp.asarray(0.5, BF16) for n in range(4)], axis=0)
    gain, bias = (jnp.concatenate([column(vector_ref[n : n + 1], LANES)] * half, axis=1) for n in range(2))
    fetch.wait()
    block = jnp.concatenate([pair_ref[row] for s in range(half) for row in (s, half + s)], axis=0)
    centered = dot(centring(chans), block, (1, 1))
    variance = jnp.mean(centered * centered, axis=0, keepdims=True)
    normed = (centered * lax.rsqrt(variance + EPS) * gain + bias).astype(BF16)
    normed_ref[...] = normed
    projected = dot(weights, normed, (1, 0))
    a_gate, a_proj, b_gate, b_proj = (projected[n * chans : (n + 1) * chans] for n in range(4))
    left, right = a_proj + jnp.tanh(a_gate) * a_proj, b_proj + jnp.tanh(b_gate) * b_proj
    pitch = 2 * half + 1
    for s in range(half):
        cut = slice(s * LANES, (s + 1) * LANES)
        wide_ref[pl.ds(s, chans, stride=pitch), :] = left[:, cut]
        wide_ref[pl.ds(half + s, chans, stride=pitch), :] = right[:, cut]
    for c in range(chans):
        out_ref[c] = wide_ref[pl.ds(c * pitch, 2 * half), :].astype(BF16)


def merge(even, odd, cols):
    return [jnp.concatenate([even[:, cut], odd[:, cut]], axis=1) for cut in (slice(0, cols), slice(cols, 2 * cols))]


def arrange_kernel(order, part, in_ref, out_ref):
    channels, rows, _, tile, depth = out_ref.shape
    lanes = in_ref.shape[3]
    count = 2 * depth // lanes
    for channel in range(channels):
        for row in range(rows):
            tiles = [in_ref[order.index(row * count + col), channel, pl.ds(part * tile, tile), :] for col in range(count)]
            for m in range(count // 2):
                for h, block in enumerate(merge(tiles[2 * m], tiles[2 * m + 1], lanes // 2)):
                    out_ref[channel, row, h, :, m * lanes : (m + 1) * lanes] = block


def gate_kernel(
    order, in_ref, normed_ref, gate_hbm, proj_hbm, gain_hbm, bias_hbm,
    out_ref, gate_ref, gain_ref, bias_ref, proj_ref, vector_ref, weight_ref, sem,
):
    copies = [pltpu.make_async_copy(ref, weight_ref.at[n], sem.at[n]) for n, ref in enumerate((gate_hbm, proj_hbm))]
    copies += [
        pltpu.make_async_copy(ref, vector_ref.at[pl.ds(n, 1)], sem.at[2 + n]) for n, ref in enumerate((gain_hbm, bias_hbm))
    ]
    start(copies)
    arrange_kernel(order, 0, in_ref, out_ref)
    wait(copies)
    gain_ref[...], bias_ref[...] = (column(vector_ref[n : n + 1], LANES) for n in range(2))
    proj_ref[...] = weight_ref[1] * jnp.asarray(0.5, BF16)
    weight = weight_ref[0] * jnp.asarray(0.5, BF16)
    half, lanes, _ = gate_ref.shape
    for s in range(half):
        gate_ref[s] = 1 + jnp.tanh(dot(normed_ref[:, s * lanes : (s + 1) * lanes], weight, (0, 0)))


def product_kernel(order, left_ref, right_ref, other_ref, out_ref):
    channels, rows, _, tile, depth = left_ref.shape
    lanes = out_ref.shape[3]
    cols, count = lanes // 2, rows * tile
    core = lax.rem(lax.axis_index("row"), 2)
    for channel in range(channels):
        own, other = right_ref[channel], other_ref[channel]
        right = jnp.stack([jnp.where(core == 0, own, other), jnp.where(core == 0, other, own)], axis=1)
        right = right.reshape(4 * count, depth)
        left = jnp.concatenate([left_ref[channel, :, h].reshape(count, depth) for h in range(2)], axis=0)
        product = dot(left, right, (1, 1)).astype(BF16)
        for m in range(4 * count // lanes):
            cut = slice(m * lanes, (m + 1) * lanes)
            for odd, block in enumerate(merge(product[:count, cut], product[count:, cut], cols)):
                for row in range(rows):
                    at = order.index(row * (4 * count // cols) + 2 * m + odd)
                    out_ref[at, channel] = block[row * tile : (row + 1) * tile]


def update_kernel(in_ref, gate_ref, gain_ref, bias_ref, weight_ref, out_hbm, wide_ref, out_ref, sem):
    chans, half, lanes = in_ref.shape
    cols = lanes // 2
    pitch = half + 1
    normed = norm(in_ref[...].astype(F32), 0)
    for c in range(chans):
        wide_ref[pl.ds(c * pitch, half), :] = normed[c]
    step = half // PARTS
    copies = []
    for s in range(half):
        mixed = (wide_ref[pl.ds(s, chans, stride=pitch), :] * gain_ref[...] + bias_ref[...]).astype(BF16)
        output = dot(mixed, weight_ref[...], (0, 0))
        update = (gate_ref[s] * output).astype(BF16)
        out_ref[s], out_ref[half + s] = update[:cols], update[cols:]
        if s % step == step - 1:
            for h in range(2):
                at = pl.ds(h * half + s - step + 1, step)
                copies += start([pltpu.make_async_copy(out_ref.at[at], out_hbm.at[at], sem.at[len(copies)])])
    wait(copies)


LANES = 128
PARTS = 4
VMEM_LIMIT = 48 * 2**20


def in_hbm(*arrays):
    return [pltpu.with_memory_space_constraint(array, pltpu.HBM) for array in arrays]


def call(kernel, out, scratch=(), flops=0, **specs):
    return pl.pallas_call(
        kernel,
        out_shape=out,
        scratch_shapes=list(scratch),
        compiler_params=pltpu.CompilerParams(vmem_limit_bytes=VMEM_LIMIT),
        cost_estimate=pl.CostEstimate(flops=flops, bytes_accessed=2**20, transcendentals=2**18),
        **specs,
    )


def per_device(
    pair, in_gain, in_bias, a_gate, a_proj, b_gate, b_proj, out_gate, mid_gain, mid_bias, out_proj
):
    rows, cols, chans = pair.shape
    hidden = a_gate.shape[1]
    row_count, col_count = lax.axis_size("row"), lax.axis_size("col")
    half, lanes = rows // 2, 2 * cols
    hbm = pl.BlockSpec(memory_space=pltpu.HBM)
    operands, normed = call(
        operands_kernel,
        (
            jax.ShapeDtypeStruct((hidden, 2 * half, lanes), BF16),
            jax.ShapeDtypeStruct((chans, rows * cols), BF16),
        ),
        [
            pltpu.VMEM(pair.shape, BF16),
            pltpu.VMEM((8, chans), F32),
            pltpu.VMEM((4, chans, hidden), BF16),
            pltpu.VMEM(((hidden + 8) * (2 * half + 1), lanes), F32),
            pltpu.SemaphoreType.DMA((7,)),
        ],
        2 * rows * cols * chans * 4 * hidden,
        in_specs=[hbm] * 7,
    )(*in_hbm(pair, in_gain[None, :], in_bias[None, :], a_gate, a_proj, b_gate, b_proj))
    order = chips(row_count, col_count)
    count, depth = row_count // 2, col_count * cols
    messages = exchange(operands.reshape(len(order), 4 * half, lanes), row_count, col_count)
    messages = messages.reshape(len(order), 2, 2 * half, lanes)
    arranged = jax.ShapeDtypeStruct((2, count, 2, half, depth), BF16)
    right = call(functools.partial(arrange_kernel, order, 1), arranged)(messages)
    other = lax.ppermute(right, "row", [(row, row ^ 1) for row in range(row_count)])
    late = jax.ShapeDtypeStruct((hidden, lanes), F32)
    left, gate, mid_gain, mid_bias, out_proj = call(
        functools.partial(gate_kernel, order),
        (
            arranged,
            jax.ShapeDtypeStruct((half, lanes, chans), F32),
            late,
            late,
            jax.ShapeDtypeStruct(out_proj.shape, BF16),
        ),
        [
            pltpu.VMEM((8, hidden), F32),
            pltpu.VMEM((2, chans, hidden), BF16),
            pltpu.SemaphoreType.DMA((4,)),
        ],
        in_specs=[pl.BlockSpec()] * 2 + [hbm] * 4,
    )(messages, normed, *in_hbm(out_gate, out_proj, mid_gain[None, :], mid_bias[None, :]))
    triangle = call(
        functools.partial(product_kernel, order),
        jax.ShapeDtypeStruct((len(order), 2, half, lanes), BF16),
        (),
        2 * 2 * (2 * count * half) * (4 * count * half) * depth,
    )(left, right, other)
    triangle = exchange(triangle.reshape(len(order), 2 * half, lanes), row_count, col_count)
    triangle = triangle.reshape(hidden, half, lanes)
    return call(
        update_kernel,
        jax.ShapeDtypeStruct(pair.shape, BF16),
        [
            pltpu.VMEM(((hidden + 8) * (half + 1), lanes), F32),
            pltpu.VMEM(pair.shape, BF16),
            pltpu.SemaphoreType.DMA((2 * PARTS,)),
        ],
        2 * rows * cols * hidden * chans,
        out_specs=hbm,
    )(triangle, gate, mid_gain, mid_bias, out_proj)


def solution(mesh):
    in_specs = (P("row", "col", None), P(), P(), P(), P(), P(), P(), P(), P(), P(), P())
    return jax.shard_map(
        per_device, mesh=mesh, in_specs=in_specs, out_specs=P("row", "col", None), check_vma=False
    )
```

```python
import functools

import jax
import jax.numpy as jnp
from jax import lax
from jax.experimental import pallas as pl
from jax.experimental.pallas import tpu as pltpu
from jax.sharding import PartitionSpec as P

BF16, F32 = jnp.bfloat16, jnp.float32
EPS = 1e-05
BOTH = ("row", "col")
FIRST = (6, 2)


def chips(row_count, col_count):
    first = FIRST[0] * col_count + FIRST[1]
    return [first] + [n for n in range(row_count // 2 * col_count) if n != first]


def exchange(values, row_count, col_count):
    devices = [
        [(2 * (n // col_count) + core) * col_count + n % col_count for n in chips(row_count, col_count)]
        for core in range(2)
    ]
    return lax.all_to_all(values, BOTH, 0, 0, axis_index_groups=devices, tiled=True)


def centring(size):
    same = lax.broadcasted_iota(jnp.int32, (size, size), 0) == lax.broadcasted_iota(jnp.int32, (size, size), 1)
    return jnp.where(same, 1 - 1 / size, -1 / size).astype(BF16)


def dot(a, b, contract):
    return lax.dot_general(a, b, ((contract[:1], contract[1:]), ((), ())), preferred_element_type=F32)


def column(vector, width):
    return jnp.broadcast_to(vector, (width, vector.shape[1])).T


def norm(values, axis):
    mean = jnp.mean(values, axis=axis, keepdims=True)
    centered = values - mean
    variance = jnp.mean(centered * centered, axis=axis, keepdims=True)
    return centered * lax.rsqrt(variance + EPS)


def start(copies):
    for copy in copies:
        copy.start()
    return copies


def wait(copies):
    for copy in copies:
        copy.wait()


def operands_kernel(
    pair_hbm, gain_hbm, bias_hbm, ag_hbm, ap_hbm, bg_hbm, bp_hbm,
    out_ref, normed_ref, pair_ref, vector_ref, weight_ref, wide_ref, sem,
):
    rows, _, chans = pair_hbm.shape
    half = rows // 2
    weights, vectors = (ag_hbm, ap_hbm, bg_hbm, bp_hbm), (gain_hbm, bias_hbm)
    small = [pltpu.make_async_copy(ref, weight_ref.at[n], sem.at[n]) for n, ref in enumerate(weights)]
    small += [
        pltpu.make_async_copy(ref, vector_ref.at[pl.ds(n, 1)], sem.at[len(weights) + n]) for n, ref in enumerate(vectors)
    ]
    fetch = pltpu.make_async_copy(pair_hbm, pair_ref, sem.at[len(small)])
    fetch.start()
    start(small)
    wait(small)
    weights = jnp.concatenate([weight_ref[n].T * jnp.asarray(0.5, BF16) for n in range(4)], axis=0)
    gain, bias = (jnp.concatenate([column(vector_ref[n : n + 1], LANES)] * half, axis=1) for n in range(2))
    fetch.wait()
    block = jnp.concatenate([pair_ref[row] for s in range(half) for row in (s, half + s)], axis=0)
    centered = dot(centring(chans), block, (1, 1))
    variance = jnp.mean(centered * centered, axis=0, keepdims=True)
    normed = (centered * lax.rsqrt(variance + EPS) * gain + bias).astype(BF16)
    normed_ref[...] = normed
    projected = dot(weights, normed, (1, 0))
    a_gate, a_proj, b_gate, b_proj = (projected[n * chans : (n + 1) * chans] for n in range(4))
    left, right = a_proj + jnp.tanh(a_gate) * a_proj, b_proj + jnp.tanh(b_gate) * b_proj
    pitch = 2 * half + 1
    for s in range(half):
        cut = slice(s * LANES, (s + 1) * LANES)
        wide_ref[pl.ds(s, chans, stride=pitch), :] = left[:, cut]
        wide_ref[pl.ds(half + s, chans, stride=pitch), :] = right[:, cut]
    for c in range(chans):
        out_ref[c] = wide_ref[pl.ds(c * pitch, 2 * half), :].astype(BF16)


def merge(even, odd, cols):
    return [jnp.concatenate([even[:, cut], odd[:, cut]], axis=1) for cut in (slice(0, cols), slice(cols, 2 * cols))]


def arrange_kernel(order, part, in_ref, out_ref):
    channels, rows, _, tile, depth = out_ref.shape
    lanes = in_ref.shape[3]
    count = 2 * depth // lanes
    for channel in range(channels):
        for row in range(rows):
            tiles = [in_ref[order.index(row * count + col), channel, pl.ds(part * tile, tile), :] for col in range(count)]
            for m in range(count // 2):
                for h, block in enumerate(merge(tiles[2 * m], tiles[2 * m + 1], lanes // 2)):
                    out_ref[channel, row, h, :, m * lanes : (m + 1) * lanes] = block


def gate_kernel(
    order, in_ref, normed_ref, gate_hbm, proj_hbm, gain_hbm, bias_hbm,
    out_ref, gate_ref, gain_ref, bias_ref, proj_ref, vector_ref, weight_ref, sem,
):
    copies = [pltpu.make_async_copy(ref, weight_ref.at[n], sem.at[n]) for n, ref in enumerate((gate_hbm, proj_hbm))]
    copies += [
        pltpu.make_async_copy(ref, vector_ref.at[pl.ds(n, 1)], sem.at[2 + n]) for n, ref in enumerate((gain_hbm, bias_hbm))
    ]
    start(copies)
    arrange_kernel(order, 0, in_ref, out_ref)
    wait(copies)
    gain_ref[...], bias_ref[...] = (column(vector_ref[n : n + 1], LANES) for n in range(2))
    proj_ref[...] = weight_ref[1] * jnp.asarray(0.5, BF16)
    weight = weight_ref[0] * jnp.asarray(0.5, BF16)
    half, lanes, _ = gate_ref.shape
    for s in range(half):
        gate_ref[s] = 1 + jnp.tanh(dot(normed_ref[:, s * lanes : (s + 1) * lanes], weight, (0, 0)))


def product_kernel(order, left_ref, right_ref, other_ref, out_ref):
    channels, rows, _, tile, depth = left_ref.shape
    lanes = out_ref.shape[3]
    cols, count = lanes // 2, rows * tile
    core = lax.rem(lax.axis_index("row"), 2)
    for channel in range(channels):
        own, other = right_ref[channel], other_ref[channel]
        right = jnp.stack([jnp.where(core == 0, own, other), jnp.where(core == 0, other, own)], axis=1)
        right = right.reshape(4 * count, depth)
        left = jnp.concatenate([left_ref[channel, :, h].reshape(count, depth) for h in range(2)], axis=0)
        product = dot(left, right, (1, 1)).astype(BF16)
        for m in range(4 * count // lanes):
            cut = slice(m * lanes, (m + 1) * lanes)
            for odd, block in enumerate(merge(product[:count, cut], product[count:, cut], cols)):
                for row in range(rows):
                    at = order.index(row * (4 * count // cols) + 2 * m + odd)
                    out_ref[at, channel] = block[row * tile : (row + 1) * tile]


def update_kernel(in_ref, gate_ref, gain_ref, bias_ref, weight_ref, out_hbm, wide_ref, out_ref, sem):
    chans, half, lanes = in_ref.shape
    cols = lanes // 2
    pitch = half + 1
    normed = norm(in_ref[...].astype(F32), 0)
    for c in range(chans):
        wide_ref[pl.ds(c * pitch, half), :] = normed[c]
    step = half // PARTS
    copies = []
    for s in range(half):
        mixed = (wide_ref[pl.ds(s, chans, stride=pitch), :] * gain_ref[...] + bias_ref[...]).astype(BF16)
        output = dot(mixed, weight_ref[...], (0, 0))
        update = (gate_ref[s] * output).astype(BF16)
        out_ref[s], out_ref[half + s] = update[:cols], update[cols:]
        if s % step == step - 1:
            for h in range(2):
                at = pl.ds(h * half + s - step + 1, step)
                copies += start([pltpu.make_async_copy(out_ref.at[at], out_hbm.at[at], sem.at[len(copies)])])
    wait(copies)


LANES = 128
PARTS = 4
VMEM_LIMIT = 48 * 2**20


def in_hbm(*arrays):
    return [pltpu.with_memory_space_constraint(array, pltpu.HBM) for array in arrays]


def call(kernel, out, scratch=(), flops=0, **specs):
    return pl.pallas_call(
        kernel,
        out_shape=out,
        scratch_shapes=list(scratch),
        compiler_params=pltpu.CompilerParams(vmem_limit_bytes=VMEM_LIMIT),
        cost_estimate=pl.CostEstimate(flops=flops, bytes_accessed=2**20, transcendentals=2**18),
        **specs,
    )


def per_device(
    pair, in_gain, in_bias, a_gate, a_proj, b_gate, b_proj, out_gate, mid_gain, mid_bias, out_proj
):
    rows, cols, chans = pair.shape
    hidden = a_gate.shape[1]
    row_count, col_count = lax.axis_size("row"), lax.axis_size("col")
    half, lanes = rows // 2, 2 * cols
    hbm = pl.BlockSpec(memory_space=pltpu.HBM)
    operands, normed = call(
        operands_kernel,
        (
            jax.ShapeDtypeStruct((hidden, 2 * half, lanes), BF16),
            jax.ShapeDtypeStruct((chans, rows * cols), BF16),
        ),
        [
            pltpu.VMEM(pair.shape, BF16),
            pltpu.VMEM((8, chans), F32),
            pltpu.VMEM((4, chans, hidden), BF16),
            pltpu.VMEM(((hidden + 8) * (2 * half + 1), lanes), F32),
            pltpu.SemaphoreType.DMA((7,)),
        ],
        2 * rows * cols * chans * 4 * hidden,
        in_specs=[hbm] * 7,
    )(*in_hbm(pair, in_gain[None, :], in_bias[None, :], a_gate, a_proj, b_gate, b_proj))
    order = chips(row_count, col_count)
    count, depth = row_count // 2, col_count * cols
    messages = exchange(operands.reshape(len(order), 4 * half, lanes), row_count, col_count)
    messages = messages.reshape(len(order), 2, 2 * half, lanes)
    arranged = jax.ShapeDtypeStruct((2, count, 2, half, depth), BF16)
    right = call(functools.partial(arrange_kernel, order, 1), arranged)(messages)
    other = lax.ppermute(right, "row", [(row, row ^ 1) for row in range(row_count)])
    late = jax.ShapeDtypeStruct((hidden, lanes), F32)
    left, gate, mid_gain, mid_bias, out_proj = call(
        functools.partial(gate_kernel, order),
        (
            arranged,
            jax.ShapeDtypeStruct((half, lanes, chans), F32),
            late,
            late,
            jax.ShapeDtypeStruct(out_proj.shape, BF16),
        ),
        [
            pltpu.VMEM((8, hidden), F32),
            pltpu.VMEM((2, chans, hidden), BF16),
            pltpu.SemaphoreType.DMA((4,)),
        ],
        in_specs=[pl.BlockSpec()] * 2 + [hbm] * 4,
    )(messages, normed, *in_hbm(out_gate, out_proj, mid_gain[None, :], mid_bias[None, :]))
    triangle = call(
        functools.partial(product_kernel, order),
        jax.ShapeDtypeStruct((len(order), 2, half, lanes), BF16),
        (),
        2 * 2 * (2 * count * half) * (4 * count * half) * depth,
    )(left, right, other)
    triangle = exchange(triangle.reshape(len(order), 2 * half, lanes), row_count, col_count)
    triangle = triangle.reshape(hidden, half, lanes)
    return call(
        update_kernel,
        jax.ShapeDtypeStruct(pair.shape, BF16),
        [
            pltpu.VMEM(((hidden + 8) * (half + 1), lanes), F32),
            pltpu.VMEM(pair.shape, BF16),
            pltpu.SemaphoreType.DMA((2 * PARTS,)),
        ],
        2 * rows * cols * hidden * chans,
        out_specs=hbm,
    )(triangle, gate, mid_gain, mid_bias, out_proj)


def solution(mesh):
    in_specs = (P("row", "col", None), P(), P(), P(), P(), P(), P(), P(), P(), P(), P())
    return jax.shard_map(
        per_device, mesh=mesh, in_specs=in_specs, out_specs=P("row", "col", None), check_vma=False
    )
```

```python
import functools

import jax
import jax.numpy as jnp
from jax import lax
from jax.experimental import pallas as pl
from jax.experimental.pallas import tpu as pltpu
from jax.sharding import PartitionSpec as P

BF16, F32 = jnp.bfloat16, jnp.float32
EPS = 1e-05
BOTH = ("row", "col")
FIRST = (6, 2)


def chips(row_count, col_count):
    first = FIRST[0] * col_count + FIRST[1]
    return [first] + [n for n in range(row_count // 2 * col_count) if n != first]


def exchange(values, row_count, col_count):
    devices = [
        [(2 * (n // col_count) + core) * col_count + n % col_count for n in chips(row_count, col_count)]
        for core in range(2)
    ]
    return lax.all_to_all(values, BOTH, 0, 0, axis_index_groups=devices, tiled=True)


def centring(size):
    same = lax.broadcasted_iota(jnp.int32, (size, size), 0) == lax.broadcasted_iota(jnp.int32, (size, size), 1)
    return jnp.where(same, 1 - 1 / size, -1 / size).astype(BF16)


def dot(a, b, contract):
    return lax.dot_general(a, b, ((contract[:1], contract[1:]), ((), ())), preferred_element_type=F32)


def column(vector, width):
    return jnp.broadcast_to(vector, (width, vector.shape[1])).T


def norm(values, axis):
    mean = jnp.mean(values, axis=axis, keepdims=True)
    centered = values - mean
    variance = jnp.mean(centered * centered, axis=axis, keepdims=True)
    return centered * lax.rsqrt(variance + EPS)


def start(copies):
    for copy in copies:
        copy.start()
    return copies


def wait(copies):
    for copy in copies:
        copy.wait()


def operands_kernel(
    pair_hbm, gain_hbm, bias_hbm, ag_hbm, ap_hbm, bg_hbm, bp_hbm,
    out_ref, normed_ref, pair_ref, vector_ref, weight_ref, wide_ref, sem,
):
    rows, _, chans = pair_hbm.shape
    half = rows // 2
    weights, vectors = (ag_hbm, ap_hbm, bg_hbm, bp_hbm), (gain_hbm, bias_hbm)
    small = [pltpu.make_async_copy(ref, weight_ref.at[n], sem.at[n]) for n, ref in enumerate(weights)]
    small += [
        pltpu.make_async_copy(ref, vector_ref.at[pl.ds(n, 1)], sem.at[len(weights) + n]) for n, ref in enumerate(vectors)
    ]
    fetch = pltpu.make_async_copy(pair_hbm, pair_ref, sem.at[len(small)])
    fetch.start()
    start(small)
    wait(small)
    weights = jnp.concatenate([weight_ref[n].T * jnp.asarray(0.5, BF16) for n in range(4)], axis=0)
    gain, bias = (jnp.concatenate([column(vector_ref[n : n + 1], LANES)] * half, axis=1) for n in range(2))
    fetch.wait()
    block = jnp.concatenate([pair_ref[row] for s in range(half) for row in (s, half + s)], axis=0)
    centered = dot(centring(chans), block, (1, 1))
    variance = jnp.mean(centered * centered, axis=0, keepdims=True)
    normed = (centered * lax.rsqrt(variance + EPS) * gain + bias).astype(BF16)
    normed_ref[...] = normed
    projected = dot(weights, normed, (1, 0))
    a_gate, a_proj, b_gate, b_proj = (projected[n * chans : (n + 1) * chans] for n in range(4))
    left, right = a_proj + jnp.tanh(a_gate) * a_proj, b_proj + jnp.tanh(b_gate) * b_proj
    pitch = 2 * half + 1
    for s in range(half):
        cut = slice(s * LANES, (s + 1) * LANES)
        wide_ref[pl.ds(s, chans, stride=pitch), :] = left[:, cut]
        wide_ref[pl.ds(half + s, chans, stride=pitch), :] = right[:, cut]
    for c in range(chans):
        out_ref[c] = wide_ref[pl.ds(c * pitch, 2 * half), :].astype(BF16)


def merge(even, odd, cols):
    return [jnp.concatenate([even[:, cut], odd[:, cut]], axis=1) for cut in (slice(0, cols), slice(cols, 2 * cols))]


def arrange_kernel(order, part, in_ref, out_ref):
    channels, rows, _, tile, depth = out_ref.shape
    lanes = in_ref.shape[3]
    count = 2 * depth // lanes
    for channel in range(channels):
        for row in range(rows):
            tiles = [in_ref[order.index(row * count + col), channel, pl.ds(part * tile, tile), :] for col in range(count)]
            for m in range(count // 2):
                for h, block in enumerate(merge(tiles[2 * m], tiles[2 * m + 1], lanes // 2)):
                    out_ref[channel, row, h, :, m * lanes : (m + 1) * lanes] = block


def gate_kernel(
    order, in_ref, normed_ref, gate_hbm, proj_hbm, gain_hbm, bias_hbm,
    out_ref, gate_ref, gain_ref, bias_ref, proj_ref, vector_ref, weight_ref, sem,
):
    copies = [pltpu.make_async_copy(ref, weight_ref.at[n], sem.at[n]) for n, ref in enumerate((gate_hbm, proj_hbm))]
    copies += [
        pltpu.make_async_copy(ref, vector_ref.at[pl.ds(n, 1)], sem.at[2 + n]) for n, ref in enumerate((gain_hbm, bias_hbm))
    ]
    start(copies)
    arrange_kernel(order, 0, in_ref, out_ref)
    wait(copies)
    gain_ref[...], bias_ref[...] = (column(vector_ref[n : n + 1], LANES) for n in range(2))
    proj_ref[...] = weight_ref[1] * jnp.asarray(0.5, BF16)
    weight = weight_ref[0] * jnp.asarray(0.5, BF16)
    half, lanes, _ = gate_ref.shape
    for s in range(half):
        gate_ref[s] = 1 + jnp.tanh(dot(normed_ref[:, s * lanes : (s + 1) * lanes], weight, (0, 0)))


def product_kernel(order, left_ref, right_ref, other_ref, out_ref):
    channels, rows, _, tile, depth = left_ref.shape
    lanes = out_ref.shape[3]
    cols, count = lanes // 2, rows * tile
    core = lax.rem(lax.axis_index("row"), 2)
    for channel in range(channels):
        own, other = right_ref[channel], other_ref[channel]
        right = jnp.stack([jnp.where(core == 0, own, other), jnp.where(core == 0, other, own)], axis=1)
        right = right.reshape(4 * count, depth)
        left = jnp.concatenate([left_ref[channel, :, h].reshape(count, depth) for h in range(2)], axis=0)
        product = dot(left, right, (1, 1))
        for m in range(4 * count // lanes):
            cut = slice(m * lanes, (m + 1) * lanes)
            for odd, block in enumerate(merge(product[:count, cut], product[count:, cut], cols)):
                for row in range(rows):
                    at = order.index(row * (4 * count // cols) + 2 * m + odd)
                    out_ref[at, channel] = block[row * tile : (row + 1) * tile]


def update_kernel(in_ref, gate_ref, gain_ref, bias_ref, weight_ref, out_hbm, wide_ref, out_ref, sem):
    chans, half, lanes = in_ref.shape
    cols = lanes // 2
    pitch = half + 1
    normed = norm(in_ref[...], 0)
    for c in range(chans):
        wide_ref[pl.ds(c * pitch, half), :] = normed[c]
    step = half // PARTS
    copies = []
    for s in range(half):
        mixed = (wide_ref[pl.ds(s, chans, stride=pitch), :] * gain_ref[...] + bias_ref[...]).astype(BF16)
        output = dot(mixed, weight_ref[...], (0, 0))
        update = (gate_ref[s] * output).astype(BF16)
        out_ref[s], out_ref[half + s] = update[:cols], update[cols:]
        if s % step == step - 1:
            for h in range(2):
                at = pl.ds(h * half + s - step + 1, step)
                copies += start([pltpu.make_async_copy(out_ref.at[at], out_hbm.at[at], sem.at[len(copies)])])
    wait(copies)


LANES = 128
PARTS = 4
VMEM_LIMIT = 48 * 2**20


def in_hbm(*arrays):
    return [pltpu.with_memory_space_constraint(array, pltpu.HBM) for array in arrays]


def call(kernel, out, scratch=(), flops=0, **specs):
    return pl.pallas_call(
        kernel,
        out_shape=out,
        scratch_shapes=list(scratch),
        compiler_params=pltpu.CompilerParams(vmem_limit_bytes=VMEM_LIMIT),
        cost_estimate=pl.CostEstimate(flops=flops, bytes_accessed=2**20, transcendentals=2**18),
        **specs,
    )


def per_device(
    pair, in_gain, in_bias, a_gate, a_proj, b_gate, b_proj, out_gate, mid_gain, mid_bias, out_proj
):
    rows, cols, chans = pair.shape
    hidden = a_gate.shape[1]
    row_count, col_count = lax.axis_size("row"), lax.axis_size("col")
    half, lanes = rows // 2, 2 * cols
    hbm = pl.BlockSpec(memory_space=pltpu.HBM)
    operands, normed = call(
        operands_kernel,
        (
            jax.ShapeDtypeStruct((hidden, 2 * half, lanes), BF16),
            jax.ShapeDtypeStruct((chans, rows * cols), BF16),
        ),
        [
            pltpu.VMEM(pair.shape, BF16),
            pltpu.VMEM((8, chans), F32),
            pltpu.VMEM((4, chans, hidden), BF16),
            pltpu.VMEM(((hidden + 8) * (2 * half + 1), lanes), F32),
            pltpu.SemaphoreType.DMA((7,)),
        ],
        2 * rows * cols * chans * 4 * hidden,
        in_specs=[hbm] * 7,
    )(*in_hbm(pair, in_gain[None, :], in_bias[None, :], a_gate, a_proj, b_gate, b_proj))
    order = chips(row_count, col_count)
    count, depth = row_count // 2, col_count * cols
    messages = exchange(operands.reshape(len(order), 4 * half, lanes), row_count, col_count)
    messages = messages.reshape(len(order), 2, 2 * half, lanes)
    arranged = jax.ShapeDtypeStruct((2, count, 2, half, depth), BF16)
    right = call(functools.partial(arrange_kernel, order, 1), arranged)(messages)
    other = lax.ppermute(right, "row", [(row, row ^ 1) for row in range(row_count)])
    late = jax.ShapeDtypeStruct((hidden, lanes), F32)
    left, gate, mid_gain, mid_bias, out_proj = call(
        functools.partial(gate_kernel, order),
        (
            arranged,
            jax.ShapeDtypeStruct((half, lanes, chans), F32),
            late,
            late,
            jax.ShapeDtypeStruct(out_proj.shape, BF16),
        ),
        [
            pltpu.VMEM((8, hidden), F32),
            pltpu.VMEM((2, chans, hidden), BF16),
            pltpu.SemaphoreType.DMA((4,)),
        ],
        in_specs=[pl.BlockSpec()] * 2 + [hbm] * 4,
    )(messages, normed, *in_hbm(out_gate, out_proj, mid_gain[None, :], mid_bias[None, :]))
    triangle = call(
        functools.partial(product_kernel, order),
        jax.ShapeDtypeStruct((len(order), 2, half, lanes), F32),
        (),
        2 * 2 * (2 * count * half) * (4 * count * half) * depth,
    )(left, right, other)
    triangle = exchange(triangle.reshape(len(order), 2 * half, lanes), row_count, col_count)
    triangle = triangle.reshape(hidden, half, lanes)
    return call(
        update_kernel,
        jax.ShapeDtypeStruct(pair.shape, BF16),
        [
            pltpu.VMEM(((hidden + 8) * (half + 1), lanes), F32),
            pltpu.VMEM(pair.shape, BF16),
            pltpu.SemaphoreType.DMA((2 * PARTS,)),
        ],
        2 * rows * cols * hidden * chans,
        out_specs=hbm,
    )(triangle, gate, mid_gain, mid_bias, out_proj)


def solution(mesh):
    in_specs = (P("row", "col", None), P(), P(), P(), P(), P(), P(), P(), P(), P(), P())
    return jax.shard_map(
        per_device, mesh=mesh, in_specs=in_specs, out_specs=P("row", "col", None), check_vma=False
    )
```

```python
import functools

import jax
import jax.numpy as jnp
from jax import lax
from jax.experimental import pallas as pl
from jax.experimental.pallas import tpu as pltpu
from jax.sharding import PartitionSpec as P

BF16, F32 = jnp.bfloat16, jnp.float32
EPS = 1e-05
BOTH = ("row", "col")
FIRST = (6, 2)


def chips(row_count, col_count):
    first = FIRST[0] * col_count + FIRST[1]
    return [first] + [n for n in range(row_count // 2 * col_count) if n != first]


def exchange(values, row_count, col_count):
    devices = [
        [(2 * (n // col_count) + core) * col_count + n % col_count for n in chips(row_count, col_count)]
        for core in range(2)
    ]
    return lax.all_to_all(values, BOTH, 0, 0, axis_index_groups=devices, tiled=True)


def dot(a, b, contract):
    return lax.dot_general(a, b, ((contract[:1], contract[1:]), ((), ())), preferred_element_type=F32)


def column(vector, width):
    return jnp.broadcast_to(vector, (width, vector.shape[1])).T


def start(copies):
    for copy in copies:
        copy.start()
    return copies


def wait(copies):
    for copy in copies:
        copy.wait()


def operands_kernel(
    pair_hbm, gain_hbm, bias_hbm, ag_hbm, ap_hbm, bg_hbm, bp_hbm,
    out_ref, normed_ref, pair_ref, vector_ref, weight_ref, wide_ref, sem,
):
    rows, _, chans = pair_hbm.shape
    half = rows // 2
    weights, vectors = (ag_hbm, ap_hbm, bg_hbm, bp_hbm), (gain_hbm, bias_hbm)
    small = [pltpu.make_async_copy(ref, weight_ref.at[n], sem.at[n]) for n, ref in enumerate(weights)]
    small += [
        pltpu.make_async_copy(ref, vector_ref.at[pl.ds(n, 1)], sem.at[len(weights) + n]) for n, ref in enumerate(vectors)
    ]
    fetch = pltpu.make_async_copy(pair_hbm, pair_ref, sem.at[len(small)])
    fetch.start()
    start(small)
    wait(small)
    fetch.wait()
    weights = jnp.concatenate([weight_ref[n].T * jnp.asarray(0.5, BF16) for n in range(4)], axis=0)
    gain, bias = (jnp.concatenate([column(vector_ref[n : n + 1], LANES)] * half, axis=1) for n in range(2))
    tiles = [jnp.concatenate([pair_ref[s], pair_ref[half + s]], axis=0).T for s in range(half)]
    turned = jnp.concatenate(tiles, axis=1).astype(F32)
    centered = turned - jnp.mean(turned, axis=0, keepdims=True)
    variance = jnp.mean(centered * centered, axis=0, keepdims=True)
    normed = (centered * lax.rsqrt(variance + EPS) * gain + bias).astype(BF16)
    normed_ref[...] = normed
    projected = dot(weights, normed, (1, 0))
    a_gate, a_proj, b_gate, b_proj = (projected[n * chans : (n + 1) * chans] for n in range(4))
    left, right = a_proj + jnp.tanh(a_gate) * a_proj, b_proj + jnp.tanh(b_gate) * b_proj
    pitch = 2 * half + 1
    for s in range(half):
        cut = slice(s * LANES, (s + 1) * LANES)
        wide_ref[pl.ds(s, chans, stride=pitch), :] = left[:, cut]
        wide_ref[pl.ds(half + s, chans, stride=pitch), :] = right[:, cut]
    for c in range(chans):
        out_ref[c] = wide_ref[pl.ds(c * pitch, 2 * half), :].astype(BF16)


def merge(even, odd, cols):
    return [jnp.concatenate([even[:, cut], odd[:, cut]], axis=1) for cut in (slice(0, cols), slice(cols, 2 * cols))]


def arrange_kernel(order, part, in_ref, out_ref):
    channels, rows, _, tile, depth = out_ref.shape
    lanes = in_ref.shape[3]
    count = 2 * depth // lanes
    for channel in range(channels):
        for row in range(rows):
            tiles = [in_ref[order.index(row * count + col), channel, pl.ds(part * tile, tile), :] for col in range(count)]
            for m in range(count // 2):
                for h, block in enumerate(merge(tiles[2 * m], tiles[2 * m + 1], lanes // 2)):
                    out_ref[channel, row, h, :, m * lanes : (m + 1) * lanes] = block


def gate_kernel(
    order, in_ref, normed_ref, gate_hbm, proj_hbm, gain_hbm, bias_hbm,
    out_ref, gate_ref, gain_ref, bias_ref, proj_ref, vector_ref, weight_ref, sem,
):
    copies = [pltpu.make_async_copy(ref, weight_ref.at[n], sem.at[n]) for n, ref in enumerate((gate_hbm, proj_hbm))]
    copies += [
        pltpu.make_async_copy(ref, vector_ref.at[pl.ds(n, 1)], sem.at[2 + n]) for n, ref in enumerate((gain_hbm, bias_hbm))
    ]
    start(copies)
    arrange_kernel(order, 0, in_ref, out_ref)
    wait(copies)
    gain_ref[...], bias_ref[...] = (column(vector_ref[n : n + 1], LANES) for n in range(2))
    proj_ref[...] = weight_ref[1] * jnp.asarray(0.5, BF16)
    weight = weight_ref[0] * jnp.asarray(0.5, BF16)
    half, lanes, _ = gate_ref.shape
    for s in range(half):
        gate_ref[s] = 1 + jnp.tanh(dot(normed_ref[:, s * lanes : (s + 1) * lanes], weight, (0, 0)))


def product_kernel(order, left_ref, right_ref, other_ref, out_ref):
    channels, rows, _, tile, depth = left_ref.shape
    lanes = out_ref.shape[3]
    cols, count = lanes // 2, rows * tile
    core = lax.rem(lax.axis_index("row"), 2)
    for channel in range(channels):
        own, other = right_ref[channel], other_ref[channel]
        right = jnp.stack([jnp.where(core == 0, own, other), jnp.where(core == 0, other, own)], axis=1)
        right = right.reshape(4 * count, depth)
        left = jnp.concatenate([left_ref[channel, :, h].reshape(count, depth) for h in range(2)], axis=0)
        product = dot(left, right, (1, 1)).astype(BF16)
        for m in range(4 * count // lanes):
            cut = slice(m * lanes, (m + 1) * lanes)
            for odd, block in enumerate(merge(product[:count, cut], product[count:, cut], cols)):
                for row in range(rows):
                    at = order.index(row * (4 * count // cols) + 2 * m + odd)
                    out_ref[at, channel] = block[row * tile : (row + 1) * tile]


def update_kernel(in_ref, gate_ref, gain_ref, bias_ref, weight_ref, out_hbm, wide_ref, out_ref, sem):
    chans, half, lanes = in_ref.shape
    cols = lanes // 2
    pitch = half + 1
    values = in_ref[...].astype(F32)
    for c in range(chans):
        wide_ref[pl.ds(c * pitch, half), :] = values[c]
    mean = jnp.mean(values, axis=0)
    centered = values - mean
    scale = lax.rsqrt(jnp.mean(centered * centered, axis=0) + EPS)
    step = half // PARTS
    copies = []
    for s in range(half):
        values = (wide_ref[pl.ds(s, chans, stride=pitch), :] - mean[s : s + 1]) * scale[s : s + 1]
        mixed = (values * gain_ref[...] + bias_ref[...]).astype(BF16)
        output = dot(mixed, weight_ref[...], (0, 0))
        update = (gate_ref[s] * output).astype(BF16)
        out_ref[s], out_ref[half + s] = update[:cols], update[cols:]
        if s % step == step - 1:
            for h in range(2):
                at = pl.ds(h * half + s - step + 1, step)
                copies += start([pltpu.make_async_copy(out_ref.at[at], out_hbm.at[at], sem.at[len(copies)])])
    wait(copies)


LANES = 128
PARTS = 4
VMEM_LIMIT = 48 * 2**20


def in_hbm(*arrays):
    return [pltpu.with_memory_space_constraint(array, pltpu.HBM) for array in arrays]


def call(kernel, out, scratch=(), flops=0, **specs):
    return pl.pallas_call(
        kernel,
        out_shape=out,
        scratch_shapes=list(scratch),
        compiler_params=pltpu.CompilerParams(vmem_limit_bytes=VMEM_LIMIT),
        cost_estimate=pl.CostEstimate(flops=flops, bytes_accessed=2**20, transcendentals=2**18),
        **specs,
    )


def per_device(
    pair, in_gain, in_bias, a_gate, a_proj, b_gate, b_proj, out_gate, mid_gain, mid_bias, out_proj
):
    rows, cols, chans = pair.shape
    hidden = a_gate.shape[1]
    row_count, col_count = lax.axis_size("row"), lax.axis_size("col")
    half, lanes = rows // 2, 2 * cols
    hbm = pl.BlockSpec(memory_space=pltpu.HBM)
    operands, normed = call(
        operands_kernel,
        (
            jax.ShapeDtypeStruct((hidden, 2 * half, lanes), BF16),
            jax.ShapeDtypeStruct((chans, rows * cols), BF16),
        ),
        [
            pltpu.VMEM(pair.shape, BF16),
            pltpu.VMEM((8, chans), F32),
            pltpu.VMEM((4, chans, hidden), BF16),
            pltpu.VMEM(((hidden + 8) * (2 * half + 1), lanes), F32),
            pltpu.SemaphoreType.DMA((7,)),
        ],
        2 * rows * cols * chans * 4 * hidden,
        in_specs=[hbm] * 7,
    )(*in_hbm(pair, in_gain[None, :], in_bias[None, :], a_gate, a_proj, b_gate, b_proj))
    order = chips(row_count, col_count)
    count, depth = row_count // 2, col_count * cols
    messages = exchange(operands.reshape(len(order), 4 * half, lanes), row_count, col_count)
    messages = messages.reshape(len(order), 2, 2 * half, lanes)
    arranged = jax.ShapeDtypeStruct((2, count, 2, half, depth), BF16)
    right = call(functools.partial(arrange_kernel, order, 1), arranged)(messages)
    other = lax.ppermute(right, "row", [(row, row ^ 1) for row in range(row_count)])
    late = jax.ShapeDtypeStruct((hidden, lanes), F32)
    left, gate, mid_gain, mid_bias, out_proj = call(
        functools.partial(gate_kernel, order),
        (
            arranged,
            jax.ShapeDtypeStruct((half, lanes, chans), F32),
            late,
            late,
            jax.ShapeDtypeStruct(out_proj.shape, BF16),
        ),
        [
            pltpu.VMEM((8, hidden), F32),
            pltpu.VMEM((2, chans, hidden), BF16),
            pltpu.SemaphoreType.DMA((4,)),
        ],
        in_specs=[pl.BlockSpec()] * 2 + [hbm] * 4,
    )(messages, normed, *in_hbm(out_gate, out_proj, mid_gain[None, :], mid_bias[None, :]))
    triangle = call(
        functools.partial(product_kernel, order),
        jax.ShapeDtypeStruct((len(order), 2, half, lanes), BF16),
        (),
        2 * 2 * (2 * count * half) * (4 * count * half) * depth,
    )(left, right, other)
    triangle = exchange(triangle.reshape(len(order), 2 * half, lanes), row_count, col_count)
    triangle = triangle.reshape(hidden, half, lanes)
    return call(
        update_kernel,
        jax.ShapeDtypeStruct(pair.shape, BF16),
        [
            pltpu.VMEM(((hidden + 8) * (half + 1), lanes), F32),
            pltpu.VMEM(pair.shape, BF16),
            pltpu.SemaphoreType.DMA((2 * PARTS,)),
        ],
        2 * rows * cols * hidden * chans,
        out_specs=hbm,
    )(triangle, gate, mid_gain, mid_bias, out_proj)


def solution(mesh):
    in_specs = (P("row", "col", None), P(), P(), P(), P(), P(), P(), P(), P(), P(), P())
    return jax.shard_map(
        per_device, mesh=mesh, in_specs=in_specs, out_specs=P("row", "col", None), check_vma=False
    )
```

```python
import functools

import jax
import jax.numpy as jnp
from jax import lax
from jax.experimental import pallas as pl
from jax.experimental.pallas import tpu as pltpu
from jax.sharding import PartitionSpec as P

BF16, F32 = jnp.bfloat16, jnp.float32
EPS = 1e-05
BOTH = ("row", "col")
FIRST = (6, 2)


def chips(row_count, col_count):
    first = FIRST[0] * col_count + FIRST[1]
    return [first] + [n for n in range(row_count // 2 * col_count) if n != first]


def exchange(values, row_count, col_count):
    devices = [
        [(2 * (n // col_count) + core) * col_count + n % col_count for n in chips(row_count, col_count)]
        for core in range(2)
    ]
    return lax.all_to_all(values, BOTH, 0, 0, axis_index_groups=devices, tiled=True)


def dot(a, b, contract):
    return lax.dot_general(a, b, ((contract[:1], contract[1:]), ((), ())), preferred_element_type=F32)


def column(vector, width):
    return jnp.broadcast_to(vector, (width, vector.shape[1])).T


def start(copies):
    for copy in copies:
        copy.start()
    return copies


def wait(copies):
    for copy in copies:
        copy.wait()


def operands_kernel(
    pair_hbm, gain_hbm, bias_hbm, ag_hbm, ap_hbm, bg_hbm, bp_hbm,
    out_ref, normed_ref, pair_ref, vector_ref, weight_ref, wide_ref, other_ref, sem,
):
    rows, _, chans = pair_hbm.shape
    half = rows // 2
    weights, vectors = (ag_hbm, ap_hbm, bg_hbm, bp_hbm), (gain_hbm, bias_hbm)
    small = [pltpu.make_async_copy(ref, weight_ref.at[n], sem.at[n]) for n, ref in enumerate(weights)]
    small += [
        pltpu.make_async_copy(ref, vector_ref.at[pl.ds(n, 1)], sem.at[len(weights) + n]) for n, ref in enumerate(vectors)
    ]
    fetch = pltpu.make_async_copy(pair_hbm, pair_ref, sem.at[len(small)])
    fetch.start()
    start(small)
    wait(small)
    fetch.wait()
    weights = jnp.concatenate([weight_ref[n].T * jnp.asarray(0.5, BF16) for n in range(4)], axis=0)
    gain, bias = (jnp.concatenate([column(vector_ref[n : n + 1], LANES)] * half, axis=1) for n in range(2))
    tiles = [jnp.concatenate([pair_ref[s], pair_ref[half + s]], axis=0).T for s in range(half)]
    turned = jnp.concatenate(tiles, axis=1).astype(F32)
    centered = turned - jnp.mean(turned, axis=0, keepdims=True)
    variance = jnp.mean(centered * centered, axis=0, keepdims=True)
    normed = (centered * lax.rsqrt(variance + EPS) * gain + bias).astype(BF16)
    normed_ref[...] = normed
    projected = dot(weights, normed, (1, 0))
    a_gate, a_proj, b_gate, b_proj = (projected[n * chans : (n + 1) * chans] for n in range(4))
    left, right = a_proj + jnp.tanh(a_gate) * a_proj, b_proj + jnp.tanh(b_gate) * b_proj
    pitch = half + 1
    for s in range(half):
        cut = slice(s * LANES, (s + 1) * LANES)
        wide_ref[pl.ds(s, chans, stride=pitch), :] = left[:, cut]
        other_ref[pl.ds(s, chans, stride=pitch), :] = right[:, cut]
    for c in range(chans):
        out_ref[c, :half] = wide_ref[pl.ds(c * pitch, half), :].astype(BF16)
        out_ref[c, half:] = other_ref[pl.ds(c * pitch, half), :].astype(BF16)


def merge(even, odd, cols):
    return [jnp.concatenate([even[:, cut], odd[:, cut]], axis=1) for cut in (slice(0, cols), slice(cols, 2 * cols))]


def arrange_kernel(order, part, in_ref, out_ref):
    channels, rows, _, tile, depth = out_ref.shape
    lanes = in_ref.shape[3]
    count = 2 * depth // lanes
    for channel in range(channels):
        for row in range(rows):
            tiles = [in_ref[order.index(row * count + col), channel, pl.ds(part * tile, tile), :] for col in range(count)]
            for m in range(count // 2):
                for h, block in enumerate(merge(tiles[2 * m], tiles[2 * m + 1], lanes // 2)):
                    out_ref[channel, row, h, :, m * lanes : (m + 1) * lanes] = block


def gate_kernel(
    order, in_ref, normed_ref, gate_hbm, proj_hbm, gain_hbm, bias_hbm,
    out_ref, gate_ref, gain_ref, bias_ref, proj_ref, vector_ref, weight_ref, sem,
):
    copies = [pltpu.make_async_copy(ref, weight_ref.at[n], sem.at[n]) for n, ref in enumerate((gate_hbm, proj_hbm))]
    copies += [
        pltpu.make_async_copy(ref, vector_ref.at[pl.ds(n, 1)], sem.at[2 + n]) for n, ref in enumerate((gain_hbm, bias_hbm))
    ]
    start(copies)
    arrange_kernel(order, 0, in_ref, out_ref)
    wait(copies)
    gain_ref[...], bias_ref[...] = (column(vector_ref[n : n + 1], LANES) for n in range(2))
    proj_ref[...] = weight_ref[1] * jnp.asarray(0.5, BF16)
    weight = weight_ref[0] * jnp.asarray(0.5, BF16)
    half, lanes, _ = gate_ref.shape
    for s in range(half):
        gate_ref[s] = 1 + jnp.tanh(dot(normed_ref[:, s * lanes : (s + 1) * lanes], weight, (0, 0)))


def product_kernel(order, left_ref, right_ref, other_ref, out_ref):
    channels, rows, _, tile, depth = left_ref.shape
    lanes = out_ref.shape[3]
    cols, count = lanes // 2, rows * tile
    core = lax.rem(lax.axis_index("row"), 2)
    for channel in range(channels):
        own, other = right_ref[channel], other_ref[channel]
        right = jnp.stack([jnp.where(core == 0, own, other), jnp.where(core == 0, other, own)], axis=1)
        right = right.reshape(4 * count, depth)
        left = jnp.concatenate([left_ref[channel, :, h].reshape(count, depth) for h in range(2)], axis=0)
        product = dot(left, right, (1, 1)).astype(BF16)
        for m in range(4 * count // lanes):
            cut = slice(m * lanes, (m + 1) * lanes)
            for odd, block in enumerate(merge(product[:count, cut], product[count:, cut], cols)):
                for row in range(rows):
                    at = order.index(row * (4 * count // cols) + 2 * m + odd)
                    out_ref[at, channel] = block[row * tile : (row + 1) * tile]


def update_kernel(in_ref, gate_ref, gain_ref, bias_ref, weight_ref, out_hbm, wide_ref, out_ref, sem):
    chans, half, lanes = in_ref.shape
    cols = lanes // 2
    pitch = half + 1
    values = in_ref[...].astype(F32)
    for c in range(chans):
        wide_ref[pl.ds(c * pitch, half), :] = values[c]
    mean = jnp.mean(values, axis=0)
    centered = values - mean
    scale = lax.rsqrt(jnp.mean(centered * centered, axis=0) + EPS)
    step = half // PARTS
    copies = []
    for s in range(half):
        values = (wide_ref[pl.ds(s, chans, stride=pitch), :] - mean[s : s + 1]) * scale[s : s + 1]
        mixed = (values * gain_ref[...] + bias_ref[...]).astype(BF16)
        output = dot(mixed, weight_ref[...], (0, 0))
        update = (gate_ref[s] * output).astype(BF16)
        out_ref[s], out_ref[half + s] = update[:cols], update[cols:]
        if s % step == step - 1:
            for h in range(2):
                at = pl.ds(h * half + s - step + 1, step)
                copies += start([pltpu.make_async_copy(out_ref.at[at], out_hbm.at[at], sem.at[len(copies)])])
    wait(copies)


LANES = 128
PARTS = 4
VMEM_LIMIT = 48 * 2**20


def in_hbm(*arrays):
    return [pltpu.with_memory_space_constraint(array, pltpu.HBM) for array in arrays]


def call(kernel, out, scratch=(), flops=0, **specs):
    return pl.pallas_call(
        kernel,
        out_shape=out,
        scratch_shapes=list(scratch),
        compiler_params=pltpu.CompilerParams(vmem_limit_bytes=VMEM_LIMIT),
        cost_estimate=pl.CostEstimate(flops=flops, bytes_accessed=2**20, transcendentals=2**18),
        **specs,
    )


def per_device(
    pair, in_gain, in_bias, a_gate, a_proj, b_gate, b_proj, out_gate, mid_gain, mid_bias, out_proj
):
    rows, cols, chans = pair.shape
    hidden = a_gate.shape[1]
    row_count, col_count = lax.axis_size("row"), lax.axis_size("col")
    half, lanes = rows // 2, 2 * cols
    hbm = pl.BlockSpec(memory_space=pltpu.HBM)
    operands, normed = call(
        operands_kernel,
        (
            jax.ShapeDtypeStruct((hidden, 2 * half, lanes), BF16),
            jax.ShapeDtypeStruct((chans, rows * cols), BF16),
        ),
        [
            pltpu.VMEM(pair.shape, BF16),
            pltpu.VMEM((8, chans), F32),
            pltpu.VMEM((4, chans, hidden), BF16),
            pltpu.VMEM(((hidden + 8) * (half + 1), lanes), F32),
            pltpu.VMEM(((hidden + 8) * (half + 1), lanes), F32),
            pltpu.SemaphoreType.DMA((7,)),
        ],
        2 * rows * cols * chans * 4 * hidden,
        in_specs=[hbm] * 7,
    )(*in_hbm(pair, in_gain[None, :], in_bias[None, :], a_gate, a_proj, b_gate, b_proj))
    order = chips(row_count, col_count)
    count, depth = row_count // 2, col_count * cols
    messages = exchange(operands.reshape(len(order), 4 * half, lanes), row_count, col_count)
    messages = messages.reshape(len(order), 2, 2 * half, lanes)
    arranged = jax.ShapeDtypeStruct((2, count, 2, half, depth), BF16)
    right = call(functools.partial(arrange_kernel, order, 1), arranged)(messages)
    other = lax.ppermute(right, "row", [(row, row ^ 1) for row in range(row_count)])
    late = jax.ShapeDtypeStruct((hidden, lanes), F32)
    left, gate, mid_gain, mid_bias, out_proj = call(
        functools.partial(gate_kernel, order),
        (
            arranged,
            jax.ShapeDtypeStruct((half, lanes, chans), F32),
            late,
            late,
            jax.ShapeDtypeStruct(out_proj.shape, BF16),
        ),
        [
            pltpu.VMEM((8, hidden), F32),
            pltpu.VMEM((2, chans, hidden), BF16),
            pltpu.SemaphoreType.DMA((4,)),
        ],
        in_specs=[pl.BlockSpec()] * 2 + [hbm] * 4,
    )(messages, normed, *in_hbm(out_gate, out_proj, mid_gain[None, :], mid_bias[None, :]))
    triangle = call(
        functools.partial(product_kernel, order),
        jax.ShapeDtypeStruct((len(order), 2, half, lanes), BF16),
        (),
        2 * 2 * (2 * count * half) * (4 * count * half) * depth,
    )(left, right, other)
    triangle = exchange(triangle.reshape(len(order), 2 * half, lanes), row_count, col_count)
    triangle = triangle.reshape(hidden, half, lanes)
    return call(
        update_kernel,
        jax.ShapeDtypeStruct(pair.shape, BF16),
        [
            pltpu.VMEM(((hidden + 8) * (half + 1), lanes), F32),
            pltpu.VMEM(pair.shape, BF16),
            pltpu.SemaphoreType.DMA((2 * PARTS,)),
        ],
        2 * rows * cols * hidden * chans,
        out_specs=hbm,
    )(triangle, gate, mid_gain, mid_bias, out_proj)


def solution(mesh):
    in_specs = (P("row", "col", None), P(), P(), P(), P(), P(), P(), P(), P(), P(), P())
    return jax.shard_map(
        per_device, mesh=mesh, in_specs=in_specs, out_specs=P("row", "col", None), check_vma=False
    )
```

```python
import functools

import jax
import jax.numpy as jnp
from jax import lax
from jax.experimental import pallas as pl
from jax.experimental.pallas import tpu as pltpu
from jax.sharding import PartitionSpec as P

BF16, F32 = jnp.bfloat16, jnp.float32
EPS = 1e-05
BOTH = ("row", "col")
FIRST = (6, 2)


def chips(row_count, col_count):
    first = FIRST[0] * col_count + FIRST[1]
    return [first] + [n for n in range(row_count // 2 * col_count) if n != first]


def exchange(values, row_count, col_count):
    devices = [
        [(2 * (n // col_count) + core) * col_count + n % col_count for n in chips(row_count, col_count)]
        for core in range(2)
    ]
    return lax.all_to_all(values, BOTH, 0, 0, axis_index_groups=devices, tiled=True)


def dot(a, b, contract):
    return lax.dot_general(a, b, ((contract[:1], contract[1:]), ((), ())), preferred_element_type=F32)


def column(vector, width):
    return jnp.broadcast_to(vector, (width, vector.shape[1])).T


def start(copies):
    for copy in copies:
        copy.start()
    return copies


def wait(copies):
    for copy in copies:
        copy.wait()


def operands_kernel(
    pair_hbm, gain_hbm, bias_hbm, ag_hbm, ap_hbm, bg_hbm, bp_hbm,
    out_ref, normed_ref, pair_ref, vector_ref, weight_ref, wide_ref, sem,
):
    rows, _, chans = pair_hbm.shape
    half = rows // 2
    weights, vectors = (ag_hbm, ap_hbm, bg_hbm, bp_hbm), (gain_hbm, bias_hbm)
    small = [pltpu.make_async_copy(ref, weight_ref.at[n], sem.at[n]) for n, ref in enumerate(weights)]
    small += [
        pltpu.make_async_copy(ref, vector_ref.at[pl.ds(n, 1)], sem.at[len(weights) + n]) for n, ref in enumerate(vectors)
    ]
    fetch = pltpu.make_async_copy(pair_hbm, pair_ref, sem.at[len(small)])
    fetch.start()
    start(small)
    wait(small)
    fetch.wait()
    weights = jnp.concatenate([weight_ref[n].T * jnp.asarray(0.5, BF16) for n in range(4)], axis=0)
    gain, bias = (jnp.concatenate([column(vector_ref[n : n + 1], LANES)] * half, axis=1) for n in range(2))
    tiles = [jnp.concatenate([pair_ref[s], pair_ref[half + s]], axis=0).T for s in range(half)]
    turned = jnp.concatenate(tiles, axis=1).astype(F32)
    centered = turned - jnp.mean(turned, axis=0, keepdims=True)
    variance = jnp.mean(centered * centered, axis=0, keepdims=True)
    normed = (centered * lax.rsqrt(variance + EPS) * gain + bias).astype(BF16)
    normed_ref[...] = normed
    projected = dot(weights, normed, (1, 0))
    a_gate, a_proj, b_gate, b_proj = (projected[n * chans : (n + 1) * chans] for n in range(4))
    left, right = a_proj + jnp.tanh(a_gate) * a_proj, b_proj + jnp.tanh(b_gate) * b_proj
    pitch = 2 * half + 1
    for s in range(half):
        cut = slice(s * LANES, (s + 1) * LANES)
        wide_ref[pl.ds(s, chans, stride=pitch), :] = left[:, cut]
        wide_ref[pl.ds(half + s, chans, stride=pitch), :] = right[:, cut]
    for c in range(chans):
        out_ref[c] = wide_ref[pl.ds(c * pitch, 2 * half), :].astype(BF16)


def merge(even, odd, cols):
    return [jnp.concatenate([even[:, cut], odd[:, cut]], axis=1) for cut in (slice(0, cols), slice(cols, 2 * cols))]


def arrange_kernel(order, part, in_ref, out_ref):
    channels, tile, depth = out_ref.shape[0], *out_ref.shape[3:]
    rows = out_ref.shape[1 + (part == 0)]
    lanes = in_ref.shape[3]
    count = 2 * depth // lanes
    for channel in range(channels):
        for row in range(rows):
            tiles = [in_ref[order.index(row * count + col), channel, pl.ds(part * tile, tile), :] for col in range(count)]
            for m in range(count // 2):
                for h, block in enumerate(merge(tiles[2 * m], tiles[2 * m + 1], lanes // 2)):
                    at = (h, row) if part == 0 else (row, h)
                    out_ref[channel, *at, :, m * lanes : (m + 1) * lanes] = block


def gate_kernel(
    order, in_ref, normed_ref, gate_hbm, proj_hbm, gain_hbm, bias_hbm,
    out_ref, gate_ref, gain_ref, bias_ref, proj_ref, vector_ref, weight_ref, sem,
):
    copies = [pltpu.make_async_copy(ref, weight_ref.at[n], sem.at[n]) for n, ref in enumerate((gate_hbm, proj_hbm))]
    copies += [
        pltpu.make_async_copy(ref, vector_ref.at[pl.ds(n, 1)], sem.at[2 + n]) for n, ref in enumerate((gain_hbm, bias_hbm))
    ]
    start(copies)
    arrange_kernel(order, 0, in_ref, out_ref)
    wait(copies)
    gain_ref[...], bias_ref[...] = (column(vector_ref[n : n + 1], LANES) for n in range(2))
    proj_ref[...] = weight_ref[1] * jnp.asarray(0.5, BF16)
    weight = weight_ref[0] * jnp.asarray(0.5, BF16)
    half, lanes, _ = gate_ref.shape
    for s in range(half):
        gate_ref[s] = 1 + jnp.tanh(dot(normed_ref[:, s * lanes : (s + 1) * lanes], weight, (0, 0)))


def product_kernel(order, left_ref, right_ref, other_ref, out_ref):
    channels, _, rows, tile, depth = left_ref.shape
    lanes = out_ref.shape[3]
    cols, count = lanes // 2, rows * tile
    core = lax.rem(lax.axis_index("row"), 2)
    for channel in range(channels):
        own, other = right_ref[channel], other_ref[channel]
        right = jnp.stack([jnp.where(core == 0, own, other), jnp.where(core == 0, other, own)], axis=1)
        right = right.reshape(4 * count, depth)
        left = left_ref[channel].reshape(2 * count, depth)
        product = dot(left, right, (1, 1)).astype(BF16)
        for m in range(4 * count // lanes):
            cut = slice(m * lanes, (m + 1) * lanes)
            for odd, block in enumerate(merge(product[:count, cut], product[count:, cut], cols)):
                for row in range(rows):
                    at = order.index(row * (4 * count // cols) + 2 * m + odd)
                    out_ref[at, channel] = block[row * tile : (row + 1) * tile]


def update_kernel(in_ref, gate_ref, gain_ref, bias_ref, weight_ref, out_hbm, wide_ref, out_ref, sem):
    chans, half, lanes = in_ref.shape
    cols = lanes // 2
    pitch = half + 1
    values = in_ref[...].astype(F32)
    for c in range(chans):
        wide_ref[pl.ds(c * pitch, half), :] = values[c]
    mean = jnp.mean(values, axis=0)
    centered = values - mean
    scale = lax.rsqrt(jnp.mean(centered * centered, axis=0) + EPS)
    step = half // PARTS
    copies = []
    for s in range(half):
        values = (wide_ref[pl.ds(s, chans, stride=pitch), :] - mean[s : s + 1]) * scale[s : s + 1]
        mixed = (values * gain_ref[...] + bias_ref[...]).astype(BF16)
        output = dot(mixed, weight_ref[...], (0, 0))
        update = (gate_ref[s] * output).astype(BF16)
        out_ref[s], out_ref[half + s] = update[:cols], update[cols:]
        if s % step == step - 1:
            for h in range(2):
                at = pl.ds(h * half + s - step + 1, step)
                copies += start([pltpu.make_async_copy(out_ref.at[at], out_hbm.at[at], sem.at[len(copies)])])
    wait(copies)


LANES = 128
PARTS = 4
VMEM_LIMIT = 48 * 2**20


def in_hbm(*arrays):
    return [pltpu.with_memory_space_constraint(array, pltpu.HBM) for array in arrays]


def call(kernel, out, scratch=(), flops=0, **specs):
    return pl.pallas_call(
        kernel,
        out_shape=out,
        scratch_shapes=list(scratch),
        compiler_params=pltpu.CompilerParams(vmem_limit_bytes=VMEM_LIMIT),
        cost_estimate=pl.CostEstimate(flops=flops, bytes_accessed=2**20, transcendentals=2**18),
        **specs,
    )


def per_device(
    pair, in_gain, in_bias, a_gate, a_proj, b_gate, b_proj, out_gate, mid_gain, mid_bias, out_proj
):
    rows, cols, chans = pair.shape
    hidden = a_gate.shape[1]
    row_count, col_count = lax.axis_size("row"), lax.axis_size("col")
    half, lanes = rows // 2, 2 * cols
    hbm = pl.BlockSpec(memory_space=pltpu.HBM)
    operands, normed = call(
        operands_kernel,
        (
            jax.ShapeDtypeStruct((hidden, 2 * half, lanes), BF16),
            jax.ShapeDtypeStruct((chans, rows * cols), BF16),
        ),
        [
            pltpu.VMEM(pair.shape, BF16),
            pltpu.VMEM((8, chans), F32),
            pltpu.VMEM((4, chans, hidden), BF16),
            pltpu.VMEM(((hidden + 8) * (2 * half + 1), lanes), F32),
            pltpu.SemaphoreType.DMA((7,)),
        ],
        2 * rows * cols * chans * 4 * hidden,
        in_specs=[hbm] * 7,
    )(*in_hbm(pair, in_gain[None, :], in_bias[None, :], a_gate, a_proj, b_gate, b_proj))
    order = chips(row_count, col_count)
    count, depth = row_count // 2, col_count * cols
    messages = exchange(operands.reshape(len(order), 4 * half, lanes), row_count, col_count)
    messages = messages.reshape(len(order), 2, 2 * half, lanes)
    arranged = jax.ShapeDtypeStruct((2, count, 2, half, depth), BF16)
    right = call(functools.partial(arrange_kernel, order, 1), arranged)(messages)
    other = lax.ppermute(right, "row", [(row, row ^ 1) for row in range(row_count)])
    late = jax.ShapeDtypeStruct((hidden, lanes), F32)
    left, gate, mid_gain, mid_bias, out_proj = call(
        functools.partial(gate_kernel, order),
        (
            jax.ShapeDtypeStruct((2, 2, count, half, depth), BF16),
            jax.ShapeDtypeStruct((half, lanes, chans), F32),
            late,
            late,
            jax.ShapeDtypeStruct(out_proj.shape, BF16),
        ),
        [
            pltpu.VMEM((8, hidden), F32),
            pltpu.VMEM((2, chans, hidden), BF16),
            pltpu.SemaphoreType.DMA((4,)),
        ],
        in_specs=[pl.BlockSpec()] * 2 + [hbm] * 4,
    )(messages, normed, *in_hbm(out_gate, out_proj, mid_gain[None, :], mid_bias[None, :]))
    triangle = call(
        functools.partial(product_kernel, order),
        jax.ShapeDtypeStruct((len(order), 2, half, lanes), BF16),
        (),
        2 * 2 * (2 * count * half) * (4 * count * half) * depth,
    )(left, right, other)
    triangle = exchange(triangle.reshape(len(order), 2 * half, lanes), row_count, col_count)
    triangle = triangle.reshape(hidden, half, lanes)
    return call(
        update_kernel,
        jax.ShapeDtypeStruct(pair.shape, BF16),
        [
            pltpu.VMEM(((hidden + 8) * (half + 1), lanes), F32),
            pltpu.VMEM(pair.shape, BF16),
            pltpu.SemaphoreType.DMA((2 * PARTS,)),
        ],
        2 * rows * cols * hidden * chans,
        out_specs=hbm,
    )(triangle, gate, mid_gain, mid_bias, out_proj)


def solution(mesh):
    in_specs = (P("row", "col", None), P(), P(), P(), P(), P(), P(), P(), P(), P(), P())
    return jax.shard_map(
        per_device, mesh=mesh, in_specs=in_specs, out_specs=P("row", "col", None), check_vma=False
    )
```

```python
import functools

import jax
import jax.numpy as jnp
from jax import lax
from jax.experimental import pallas as pl
from jax.experimental.pallas import tpu as pltpu
from jax.sharding import PartitionSpec as P

BF16, F32 = jnp.bfloat16, jnp.float32
EPS = 1e-05
BOTH = ("row", "col")
FIRST = (6, 2)


def chips(row_count, col_count):
    first = FIRST[0] * col_count + FIRST[1]
    return [first] + [n for n in range(row_count // 2 * col_count) if n != first]


def exchange(values, row_count, col_count):
    devices = [
        [(2 * (n // col_count) + core) * col_count + n % col_count for n in chips(row_count, col_count)]
        for core in range(2)
    ]
    return lax.all_to_all(values, BOTH, 0, 0, axis_index_groups=devices, tiled=True)


def dot(a, b, contract):
    return lax.dot_general(a, b, ((contract[:1], contract[1:]), ((), ())), preferred_element_type=F32)


def column(vector, width):
    return jnp.broadcast_to(vector, (width, vector.shape[1])).T


def start(copies):
    for copy in copies:
        copy.start()
    return copies


def wait(copies):
    for copy in copies:
        copy.wait()


def operands_kernel(
    pair_hbm, gain_hbm, bias_hbm, ag_hbm, ap_hbm, bg_hbm, bp_hbm,
    out_ref, normed_ref, pair_ref, vector_ref, weight_ref, wide_ref, sem,
):
    rows, _, chans = pair_hbm.shape
    half = rows // 2
    weights, vectors = (ag_hbm, ap_hbm, bg_hbm, bp_hbm), (gain_hbm, bias_hbm)
    small = [pltpu.make_async_copy(ref, weight_ref.at[n], sem.at[n]) for n, ref in enumerate(weights)]
    small += [
        pltpu.make_async_copy(ref, vector_ref.at[pl.ds(n, 1)], sem.at[len(weights) + n]) for n, ref in enumerate(vectors)
    ]
    fetch = pltpu.make_async_copy(pair_hbm, pair_ref, sem.at[len(small)])
    fetch.start()
    start(small)
    wait(small)
    fetch.wait()
    weights = jnp.concatenate([weight_ref[n].T * jnp.asarray(0.5, BF16) for n in range(4)], axis=0)
    gain, bias = (jnp.concatenate([column(vector_ref[n : n + 1], LANES)] * half, axis=1) for n in range(2))
    tiles = [jnp.concatenate([pair_ref[s], pair_ref[half + s]], axis=0).T for s in range(half)]
    turned = jnp.concatenate(tiles, axis=1).astype(F32)
    centered = turned - jnp.mean(turned, axis=0, keepdims=True)
    variance = jnp.mean(centered * centered, axis=0, keepdims=True)
    normed = (centered * lax.rsqrt(variance + EPS) * gain + bias).astype(BF16)
    normed_ref[...] = normed
    projected = dot(weights, normed, (1, 0))
    a_gate, a_proj, b_gate, b_proj = (projected[n * chans : (n + 1) * chans] for n in range(4))
    left, right = a_proj + jnp.tanh(a_gate) * a_proj, b_proj + jnp.tanh(b_gate) * b_proj
    pitch = 2 * half + 1
    for s in range(half):
        cut = slice(s * LANES, (s + 1) * LANES)
        wide_ref[pl.ds(s, chans, stride=pitch), :] = left[:, cut]
        wide_ref[pl.ds(half + s, chans, stride=pitch), :] = right[:, cut]
    for c in range(chans):
        out_ref[c] = wide_ref[pl.ds(c * pitch, 2 * half), :].astype(BF16)


def merge(even, odd, cols):
    return [jnp.concatenate([even[:, cut], odd[:, cut]], axis=1) for cut in (slice(0, cols), slice(cols, 2 * cols))]


def arrange_kernel(order, part, in_ref, out_ref):
    channels, rows, _, tile, depth = out_ref.shape
    lanes = in_ref.shape[3]
    count = 2 * depth // lanes
    for channel in range(channels):
        for row in range(rows):
            tiles = [in_ref[order.index(row * count + col), channel, pl.ds(part * tile, tile), :] for col in range(count)]
            for m in range(count // 2):
                for h, block in enumerate(merge(tiles[2 * m], tiles[2 * m + 1], lanes // 2)):
                    out_ref[channel, row, h, :, m * lanes : (m + 1) * lanes] = block


def gate_kernel(
    order, in_ref, normed_ref, gate_hbm, proj_hbm, gain_hbm, bias_hbm,
    out_ref, gate_ref, gain_ref, bias_ref, proj_ref, vector_ref, weight_ref, sem,
):
    copies = [pltpu.make_async_copy(ref, weight_ref.at[n], sem.at[n]) for n, ref in enumerate((gate_hbm, proj_hbm))]
    copies += [
        pltpu.make_async_copy(ref, vector_ref.at[pl.ds(n, 1)], sem.at[2 + n]) for n, ref in enumerate((gain_hbm, bias_hbm))
    ]
    start(copies)
    arrange_kernel(order, 0, in_ref, out_ref)
    wait(copies)
    gain_ref[...], bias_ref[...] = (column(vector_ref[n : n + 1], LANES) for n in range(2))
    proj_ref[...] = weight_ref[1] * jnp.asarray(0.5, BF16)
    weight = weight_ref[0] * jnp.asarray(0.5, BF16)
    half, lanes, _ = gate_ref.shape
    for s in range(half):
        gate_ref[s] = 1 + jnp.tanh(dot(normed_ref[:, s * lanes : (s + 1) * lanes], weight, (0, 0)))


def product_kernel(order, left_ref, right_ref, other_ref, out_ref):
    channels, rows, _, tile, depth = left_ref.shape
    lanes = out_ref.shape[3]
    cols, count = lanes // 2, rows * tile
    core = lax.rem(lax.axis_index("row"), 2)
    for channel in range(channels):
        own, other = right_ref[channel], other_ref[channel]
        right = jnp.stack([jnp.where(core == 0, own, other), jnp.where(core == 0, other, own)], axis=1)
        right = right.reshape(4 * count, depth)
        left = jnp.concatenate([left_ref[channel, :, h].reshape(count, depth) for h in range(2)], axis=0)
        product = dot(left, right, (1, 1)).astype(BF16)
        for m in range(4 * count // lanes):
            cut = slice(m * lanes, (m + 1) * lanes)
            for odd, block in enumerate(merge(product[:count, cut], product[count:, cut], cols)):
                for row in range(rows):
                    at = order.index(row * (4 * count // cols) + 2 * m + odd)
                    out_ref[at, channel] = block[row * tile : (row + 1) * tile]


def update_kernel(in_ref, gate_ref, gain_ref, bias_ref, weight_ref, out_hbm, wide_ref, out_ref, sem):
    chans, half, lanes = in_ref.shape
    cols = lanes // 2
    pitch = half + 1
    values = in_ref[...].astype(F32)
    for c in range(chans):
        wide_ref[pl.ds(c * pitch, half), :] = values[c]
    mean = jnp.mean(values, axis=0)
    centered = values - mean
    scale = lax.rsqrt(jnp.mean(centered * centered, axis=0) + EPS)
    step = half // PARTS
    copies = []
    for s in range(half):
        values = (wide_ref[pl.ds(s, chans, stride=pitch), :] - mean[s : s + 1]) * scale[s : s + 1]
        mixed = (values * gain_ref[...] + bias_ref[...]).astype(BF16)
        output = dot(mixed, weight_ref[...], (0, 0))
        update = (gate_ref[s] * output).astype(BF16)
        out_ref[s], out_ref[half + s] = update[:cols], update[cols:]
        if s % step == step - 1:
            for h in range(2):
                at = pl.ds(h * half + s - step + 1, step)
                copies += start([pltpu.make_async_copy(out_ref.at[at], out_hbm.at[at], sem.at[len(copies)])])
    wait(copies)


LANES = 128
PARTS = 2
VMEM_LIMIT = 48 * 2**20


def in_hbm(*arrays):
    return [pltpu.with_memory_space_constraint(array, pltpu.HBM) for array in arrays]


def call(kernel, out, scratch=(), flops=0, **specs):
    return pl.pallas_call(
        kernel,
        out_shape=out,
        scratch_shapes=list(scratch),
        compiler_params=pltpu.CompilerParams(vmem_limit_bytes=VMEM_LIMIT),
        cost_estimate=pl.CostEstimate(flops=flops, bytes_accessed=2**20, transcendentals=2**18),
        **specs,
    )


def per_device(
    pair, in_gain, in_bias, a_gate, a_proj, b_gate, b_proj, out_gate, mid_gain, mid_bias, out_proj
):
    rows, cols, chans = pair.shape
    hidden = a_gate.shape[1]
    row_count, col_count = lax.axis_size("row"), lax.axis_size("col")
    half, lanes = rows // 2, 2 * cols
    hbm = pl.BlockSpec(memory_space=pltpu.HBM)
    operands, normed = call(
        operands_kernel,
        (
            jax.ShapeDtypeStruct((hidden, 2 * half, lanes), BF16),
            jax.ShapeDtypeStruct((chans, rows * cols), BF16),
        ),
        [
            pltpu.VMEM(pair.shape, BF16),
            pltpu.VMEM((8, chans), F32),
            pltpu.VMEM((4, chans, hidden), BF16),
            pltpu.VMEM(((hidden + 8) * (2 * half + 1), lanes), F32),
            pltpu.SemaphoreType.DMA((7,)),
        ],
        2 * rows * cols * chans * 4 * hidden,
        in_specs=[hbm] * 7,
    )(*in_hbm(pair, in_gain[None, :], in_bias[None, :], a_gate, a_proj, b_gate, b_proj))
    order = chips(row_count, col_count)
    count, depth = row_count // 2, col_count * cols
    messages = exchange(operands.reshape(len(order), 4 * half, lanes), row_count, col_count)
    messages = messages.reshape(len(order), 2, 2 * half, lanes)
    arranged = jax.ShapeDtypeStruct((2, count, 2, half, depth), BF16)
    right = call(functools.partial(arrange_kernel, order, 1), arranged)(messages)
    other = lax.ppermute(right, "row", [(row, row ^ 1) for row in range(row_count)])
    late = jax.ShapeDtypeStruct((hidden, lanes), F32)
    left, gate, mid_gain, mid_bias, out_proj = call(
        functools.partial(gate_kernel, order),
        (
            arranged,
            jax.ShapeDtypeStruct((half, lanes, chans), F32),
            late,
            late,
            jax.ShapeDtypeStruct(out_proj.shape, BF16),
        ),
        [
            pltpu.VMEM((8, hidden), F32),
            pltpu.VMEM((2, chans, hidden), BF16),
            pltpu.SemaphoreType.DMA((4,)),
        ],
        in_specs=[pl.BlockSpec()] * 2 + [hbm] * 4,
    )(messages, normed, *in_hbm(out_gate, out_proj, mid_gain[None, :], mid_bias[None, :]))
    triangle = call(
        functools.partial(product_kernel, order),
        jax.ShapeDtypeStruct((len(order), 2, half, lanes), BF16),
        (),
        2 * 2 * (2 * count * half) * (4 * count * half) * depth,
    )(left, right, other)
    triangle = exchange(triangle.reshape(len(order), 2 * half, lanes), row_count, col_count)
    triangle = triangle.reshape(hidden, half, lanes)
    return call(
        update_kernel,
        jax.ShapeDtypeStruct(pair.shape, BF16),
        [
            pltpu.VMEM(((hidden + 8) * (half + 1), lanes), F32),
            pltpu.VMEM(pair.shape, BF16),
            pltpu.SemaphoreType.DMA((2 * PARTS,)),
        ],
        2 * rows * cols * hidden * chans,
        out_specs=hbm,
    )(triangle, gate, mid_gain, mid_bias, out_proj)


def solution(mesh):
    in_specs = (P("row", "col", None), P(), P(), P(), P(), P(), P(), P(), P(), P(), P())
    return jax.shard_map(
        per_device, mesh=mesh, in_specs=in_specs, out_specs=P("row", "col", None), check_vma=False
    )
```
